32 devices in a mesh: wide: 16 (over z, x, core), narrow: 2 (over y).
Axes of the slice: x: 2, y: 2, z: 4, core: 2. Of those that a mesh axis runs over, the one named last changes fastest.
Arguments:
- spectra: bfloat16 [96, 2, 2, 4096], P('wide', None, None, 'narrow'), may hold values from -6 to 6
- dead_mask: int32 [96], P('wide'), may hold values 0 or 1
- seg_offsets: int32 [96, 2], P('wide'), may hold values from 0 to 32767
- src_index: int32 [64], replicated, may hold values from 0 to 95, as said below
Outputs:
- correlations: float32 [64, 96, 512], P('narrow', 'wide')
The draws below stay inside these ranges and needn't reach their ends.
Inputs may be any that keep to these rules, and one draw needn't show every extreme that they name: `src_index`: source j is one of the 6 channels j // 4 * 6 to j // 4 * 6 + 5; the 4 sources of one block are distinct; source 0 is channel 0 and source 64 - 4 is channel 96 - 1.
All inputs are finite; a program needn't handle non-finite values. No bound on the sum of `dead_mask` on one device may be relied on, other than what follows from the above.
Results may differ from the reference program's by a relative error of at most 0.0013.
Values may be sent and summed in bfloat16 or wider, within the bound.
A program may use at most 128 MiB of HBM per device.

```python
import math
import jax
import jax.numpy as jnp
from jax import lax

CH_DEV = 6
SEGS = 2
FREQS = 4096
NSAMP = 32768
LAGS = 512
SMOOTH = 64
SG = 4
SOURCES = 64
CHANNELS = 96


def block_choice(subkey, target):
    order = jax.random.permutation(subkey, CH_DEV).astype(jnp.int32)
    where_at = jnp.argmax(order == target).astype(jnp.int32)
    first = order[0]
    swapped = order.at[where_at].set(first).at[0].set(target)
    return jnp.where(target >= 0, swapped, order)[:SG]


def draw_src_index(key, part):
    key = jax.random.fold_in(key, 11)
    blocks = SOURCES // SG
    subkeys = jax.random.split(key, blocks)
    block_ids = jnp.arange(blocks, dtype=jnp.int32)
    targets = jnp.where(block_ids == 0, 0, jnp.where(block_ids == blocks - 1, CH_DEV - 1, -1)).astype(jnp.int32)
    chosen = jax.vmap(block_choice)(subkeys, targets).astype(jnp.int32)
    offset_rows = (block_ids * CH_DEV)[:, None]
    return (offset_rows + chosen).reshape(SOURCES)


def place_ends(drawn, rng, least, high):
    dims = drawn.shape
    place = [jax.random.randint(jax.random.fold_in(rng, axis), (), 0, dims[axis]) for axis in range(len(dims))]
    drawn = drawn.at[tuple(place)].set(least)
    longest = dims.index(max(dims))
    place[longest] = (place[longest] + 1) % dims[longest]
    return drawn.at[tuple(place)].set(high)


def block_scale(stream_key, dims, cuts, low, top_value):
    gain, own = 1.0, jax.random.fold_in(stream_key, 6)
    for axis_at, parts in cuts:
        steps = jnp.exp(jax.random.uniform(jax.random.fold_in(own, axis_at), (parts,), jnp.float32, low / len(cuts), top_value / len(cuts)))
        gain = gain * jnp.repeat(steps, dims[axis_at] // parts).reshape([-1 if axis == axis_at else 1 for axis in range(len(dims))])
    return gain


def normal_values(key, extent, scale, bound, shards=(), held_as=jnp.bfloat16):
    entries = scale * jax.random.normal(key, extent, jnp.float32)
    if shards:
        entries = entries * block_scale(key, extent, shards, -0.22, 0.18)
    return jnp.clip(entries, -bound, bound).astype(held_as)


def setup_inputs(seed: int = 0) -> dict:
    keys = jax.random.split(jax.random.key(seed), 5)
    spectra = normal_values(keys[0], (CHANNELS, SEGS, 2, FREQS), 1.0, 6.0, ((0, 16), (3, 2)))
    dead_mask = place_ends((jax.random.randint(keys[1], (CHANNELS,), 0, 8) < 7).astype(jnp.int32), jax.random.fold_in(keys[1], 1), 0, 1)
    seg_offsets = place_ends(jax.random.randint(keys[2], (CHANNELS, SEGS), 0, NSAMP), jax.random.fold_in(keys[2], 1), 0, NSAMP - 1).astype(jnp.int32)
    src_index = draw_src_index(jax.random.fold_in(keys[4], 71), 0)
    return {"spectra": spectra, "dead_mask": dead_mask, "seg_offsets": seg_offsets, "src_index": src_index}


EPSILON = 1e-06

def lag_table(first, length, lag_count):
    bins = first + jnp.arange(length, dtype=jnp.int32) + 1
    lag_steps = jnp.arange(lag_count, dtype=jnp.int32) - lag_count // 2 + NSAMP
    residue = bins[:, None] * lag_steps[None, :] % NSAMP
    angles = 2.0 * math.pi / NSAMP * residue.astype(jnp.float32)
    return jnp.concatenate([jnp.cos(angles), -jnp.sin(angles)], axis=0).astype(jnp.bfloat16)

def apply_whitening(real_part, imag_part, windowed, freq_bins, total_bins, dead_mask, seg_offsets):
    counts = (jnp.minimum(freq_bins + SMOOTH, total_bins - 1) - jnp.maximum(freq_bins - SMOOTH, 0) + 1).astype(jnp.float32)
    smoothed = windowed / counts + EPSILON
    residue = (freq_bins + 1)[None, None, :] * seg_offsets[:, :, None] % NSAMP
    phase = 2.0 * math.pi / NSAMP * residue.astype(jnp.float32)
    scale = dead_mask.astype(jnp.float32)[:, None, None] / smoothed
    cosine = jnp.cos(phase)
    sine = jnp.sin(phase)
    white_real = (real_part * cosine - imag_part * sine) * scale
    white_imag = (real_part * sine + imag_part * cosine) * scale
    return jnp.stack([white_real, white_imag], axis=2).astype(jnp.bfloat16)

def cross_spectra(channels, sources, seg_count):
    chan_real = channels[:, :, 0].astype(jnp.float32)
    chan_imag = channels[:, :, 1].astype(jnp.float32)
    src_real = sources[:, :, 0].astype(jnp.float32)
    src_imag = sources[:, :, 1].astype(jnp.float32)
    cross_real = jnp.einsum('ckf,skf->scf', chan_real, src_real) + jnp.einsum('ckf,skf->scf', chan_imag, src_imag)
    cross_imag = jnp.einsum('ckf,skf->scf', chan_imag, src_real) - jnp.einsum('ckf,skf->scf', chan_real, src_imag)
    joined = jnp.concatenate([cross_real, cross_imag], axis=-1) * (1.0 / math.sqrt(seg_count))
    return joined.astype(jnp.bfloat16)

def reference(spectra, dead_mask, seg_offsets, src_index):
    seg_count = spectra.shape[1]
    total_bins = spectra.shape[3]
    real_part = spectra[:, :, 0].astype(jnp.float32)
    imag_part = spectra[:, :, 1].astype(jnp.float32)
    amplitude = jnp.sqrt(real_part * real_part + imag_part * imag_part)
    padded = jnp.pad(amplitude, ((0, 0), (0, 0), (SMOOTH, SMOOTH)))
    windowed = lax.reduce_window(padded, jnp.zeros((), padded.dtype), lax.add, (1, 1, 2 * SMOOTH + 1), (1, 1, 1), 'VALID')
    freq_bins = jnp.arange(total_bins, dtype=jnp.int32)
    whitened = apply_whitening(real_part, imag_part, windowed, freq_bins, total_bins, dead_mask, seg_offsets)
    panel = whitened[src_index.astype(jnp.int32)]
    table = lag_table(0, total_bins, LAGS)

    def one_source(source):
        spectra_x = cross_spectra(whitened, source[None], seg_count)[0]
        return jnp.dot(spectra_x, table, preferred_element_type=jnp.float32) / math.sqrt(total_bins)
    return lax.map(one_source, panel)
```

```python
import math

import jax
import jax.numpy as jnp
from jax import lax
from jax.sharding import PartitionSpec as P

NSAMP = 32768
LAGS = 512
SMOOTH = 64


EPSILON = 1e-06


def padded_2(cells, sides, width):
    for axis, dim in sides:
        count = lax.axis_size(axis)
        ends = count - 1
        head = lax.slice_in_dim(cells, 0, width, axis=dim)
        tail = lax.slice_in_dim(cells, cells.shape[dim] - width, cells.shape[dim], axis=dim)
        cells = jnp.concatenate(
            [
                lax.ppermute(tail, axis, [(i, (i + 1) % count) for i in range(ends)]),
                cells,
                lax.ppermute(head, axis, [((i + 1) % count, i) for i in range(ends)]),
            ],
            axis=dim,
        )
    return cells


def window_sums(padded, bins):
    step = 2 * SMOOTH
    blocks = bins // step
    head = padded[..., :bins].reshape(padded.shape[:-1] + (blocks, step))
    tail = padded[..., step:].reshape(padded.shape[:-1] + (blocks, step))
    cells = jnp.concatenate([head, tail], axis=-1)
    ahead = jnp.arange(2 * step)[:, None] - jnp.arange(step)[None, :]
    band = ((ahead >= 0) & (ahead <= step)).astype(jnp.float32)
    sums = jnp.einsum("ckbi,io->ckbo", cells, band, precision=lax.Precision.HIGHEST)
    return sums.reshape(padded.shape[:-1] + (bins,))


def turns(product):
    angles = 2.0 * math.pi / NSAMP * (product % NSAMP).astype(jnp.float32)
    return jnp.cos(angles), jnp.sin(angles)


def lag_table(first, length, lag_count):
    step = 128
    lag_steps = jnp.arange(lag_count, dtype=jnp.int32) - lag_count // 2 + NSAMP
    coarse = first + step * jnp.arange(length // step, dtype=jnp.int32)
    fine = jnp.arange(step, dtype=jnp.int32) + 1
    ca, sa = turns(coarse[:, None] * lag_steps[None, :])
    cb, sb = turns(fine[:, None] * lag_steps[None, :])
    cosine = ca[:, None] * cb[None] - sa[:, None] * sb[None]
    sine = sa[:, None] * cb[None] + ca[:, None] * sb[None]
    return jnp.concatenate(
        [cosine.reshape(length, lag_count), -sine.reshape(length, lag_count)], axis=0
    ).astype(jnp.bfloat16)


def apply_whitening(real_part, imag_part, windowed, freq_bins, total_bins, dead_mask, seg_offsets):
    counts = (
        jnp.minimum(freq_bins + SMOOTH, total_bins - 1) - jnp.maximum(freq_bins - SMOOTH, 0) + 1
    ).astype(jnp.float32)
    smoothed = windowed / counts + EPSILON
    residue = (freq_bins + 1)[None, None, :] * seg_offsets[:, :, None] % NSAMP
    phase = 2.0 * math.pi / NSAMP * residue.astype(jnp.float32)
    scale = dead_mask.astype(jnp.float32)[:, None, None] / smoothed
    cosine = jnp.cos(phase)
    sine = jnp.sin(phase)
    white_real = (real_part * cosine - imag_part * sine) * scale
    white_imag = (real_part * sine + imag_part * cosine) * scale
    return jnp.stack([white_real, white_imag], axis=2).astype(jnp.bfloat16)


def cross_spectra(channels, sources, seg_count):
    chan_real = channels[:, :, 0]
    chan_imag = channels[:, :, 1]
    src_real = sources[:, :, 0]
    src_imag = sources[:, :, 1]
    cross_real = jnp.einsum(
        "ckf,skf->scf", chan_real, src_real, preferred_element_type=jnp.float32
    ) + jnp.einsum("ckf,skf->scf", chan_imag, src_imag, preferred_element_type=jnp.float32)
    cross_imag = jnp.einsum(
        "ckf,skf->scf", chan_imag, src_real, preferred_element_type=jnp.float32
    ) - jnp.einsum("ckf,skf->scf", chan_real, src_imag, preferred_element_type=jnp.float32)
    joined = jnp.concatenate([cross_real, cross_imag], axis=-1) * (1.0 / math.sqrt(seg_count))
    return joined.astype(jnp.bfloat16)


def body(spectra, dead_mask, seg_offsets, src_index):
    ch_count = spectra.shape[0]
    seg_count = spectra.shape[1]
    slice_bins = spectra.shape[3]
    narrow_count = lax.axis_size("narrow")
    wide_count = lax.axis_size("wide")
    total_bins = slice_bins * narrow_count
    narrow_pos = lax.axis_index("narrow")
    wide_pos = lax.axis_index("wide")
    freq_bins = narrow_pos * slice_bins + jnp.arange(slice_bins, dtype=jnp.int32)
    real_part = spectra[:, :, 0].astype(jnp.float32)
    imag_part = spectra[:, :, 1].astype(jnp.float32)
    amplitude = jnp.sqrt(real_part * real_part + imag_part * imag_part)
    padded = padded_2(amplitude, (("narrow", 2),), SMOOTH)
    windowed = window_sums(padded, slice_bins)
    whitened = apply_whitening(
        real_part, imag_part, windowed, freq_bins, total_bins, dead_mask, seg_offsets
    )
    per_block = src_index.shape[0] // wide_count
    own_rows = (
        lax.dynamic_slice_in_dim(src_index, wide_pos * per_block, per_block) - wide_pos * ch_count
    )
    selector = (own_rows[:, None] == jnp.arange(ch_count, dtype=jnp.int32)[None, :]).astype(
        jnp.bfloat16
    )
    chosen = jnp.einsum(
        "rc,ckqf->rkqf", selector, whitened, preferred_element_type=jnp.float32
    ).astype(jnp.bfloat16)
    share_rows = src_index.shape[0] // narrow_count
    norm_factor = 1.0 / math.sqrt(total_bins)
    panel = lax.all_gather(chosen, "wide", axis=0, tiled=True)
    table_part = lag_table(narrow_pos * slice_bins, slice_bins, LAGS)
    block = lax.slice_in_dim(panel, 0, share_rows * lax.axis_size("narrow"), axis=0)
    spectra_x = cross_spectra(whitened, block, seg_count)
    flat = spectra_x.reshape(share_rows * lax.axis_size("narrow") * ch_count, 2 * slice_bins)
    product = jnp.dot(flat, table_part, preferred_element_type=jnp.float32) * norm_factor
    return lax.psum_scatter(
        product.reshape(share_rows * lax.axis_size("narrow"), ch_count, LAGS),
        "narrow",
        scatter_dimension=0,
        tiled=True,
    )


def solution(mesh):
    placed = (P("wide", None, None, "narrow"), P("wide"), P("wide", None), P())
    return jax.shard_map(
        body, mesh=mesh, in_specs=placed, out_specs=P("narrow", "wide", None), check_vma=False
    )
```

```python
import math

import jax
import jax.numpy as jnp
from jax import lax
from jax.experimental import pallas as pl
from jax.experimental.pallas import tpu as pltpu
from jax.sharding import PartitionSpec as P

NSAMP = 32768
LAGS = 512
SMOOTH = 64


EPSILON = 1e-06
MESH = pl.DeviceIdType.MESH


def padded_2(cells, sides, width):
    for axis, dim in sides:
        count = lax.axis_size(axis)
        ends = count - 1
        head = lax.slice_in_dim(cells, 0, width, axis=dim)
        tail = lax.slice_in_dim(cells, cells.shape[dim] - width, cells.shape[dim], axis=dim)
        cells = jnp.concatenate(
            [
                lax.ppermute(tail, axis, [(i, (i + 1) % count) for i in range(ends)]),
                cells,
                lax.ppermute(head, axis, [((i + 1) % count, i) for i in range(ends)]),
            ],
            axis=dim,
        )
    return cells


def window_sums(padded, bins):
    step = 2 * SMOOTH
    blocks = bins // step
    head = padded[..., :bins].reshape(padded.shape[:-1] + (blocks, step))
    tail = padded[..., step:].reshape(padded.shape[:-1] + (blocks, step))
    cells = jnp.concatenate([head, tail], axis=-1)
    ahead = jnp.arange(2 * step)[:, None] - jnp.arange(step)[None, :]
    band = ((ahead >= 0) & (ahead <= step)).astype(jnp.float32)
    sums = jnp.einsum("ckbi,io->ckbo", cells, band, precision=lax.Precision.HIGHEST)
    return sums.reshape(padded.shape[:-1] + (bins,))


def turns(product):
    angles = 2.0 * math.pi / NSAMP * (product % NSAMP).astype(jnp.float32)
    return jnp.cos(angles), jnp.sin(angles)


def lag_table(first, length, lag_count):
    step = 128
    lag_steps = jnp.arange(lag_count, dtype=jnp.int32) - lag_count // 2 + NSAMP
    coarse = first + step * jnp.arange(length // step, dtype=jnp.int32)
    fine = jnp.arange(step, dtype=jnp.int32) + 1
    ca, sa = turns(coarse[:, None] * lag_steps[None, :])
    cb, sb = turns(fine[:, None] * lag_steps[None, :])
    cosine = ca[:, None] * cb[None] - sa[:, None] * sb[None]
    sine = sa[:, None] * cb[None] + ca[:, None] * sb[None]
    return jnp.concatenate(
        [cosine.reshape(length, lag_count), -sine.reshape(length, lag_count)], axis=0
    ).astype(jnp.bfloat16)


def apply_whitening(real_part, imag_part, windowed, freq_bins, total_bins, dead_mask, seg_offsets):
    counts = (
        jnp.minimum(freq_bins + SMOOTH, total_bins - 1) - jnp.maximum(freq_bins - SMOOTH, 0) + 1
    ).astype(jnp.float32)
    smoothed = windowed / counts + EPSILON
    residue = (freq_bins + 1)[None, None, :] * seg_offsets[:, :, None] % NSAMP
    phase = 2.0 * math.pi / NSAMP * residue.astype(jnp.float32)
    scale = dead_mask.astype(jnp.float32)[:, None, None] / smoothed
    cosine = jnp.cos(phase)
    sine = jnp.sin(phase)
    white_real = (real_part * cosine - imag_part * sine) * scale
    white_imag = (real_part * sine + imag_part * cosine) * scale
    return jnp.stack([white_real, white_imag], axis=2).astype(jnp.bfloat16)


def cross_spectra(channels, sources, seg_count):
    chan_real = channels[:, :, 0]
    chan_imag = channels[:, :, 1]
    src_real = sources[:, :, 0]
    src_imag = sources[:, :, 1]
    cross_real = jnp.einsum(
        "ckf,skf->scf", chan_real, src_real, preferred_element_type=jnp.float32
    ) + jnp.einsum("ckf,skf->scf", chan_imag, src_imag, preferred_element_type=jnp.float32)
    cross_imag = jnp.einsum(
        "ckf,skf->scf", chan_imag, src_real, preferred_element_type=jnp.float32
    ) - jnp.einsum("ckf,skf->scf", chan_real, src_imag, preferred_element_type=jnp.float32)
    joined = jnp.concatenate([cross_real, cross_imag], axis=-1) * (1.0 / math.sqrt(seg_count))
    return joined.astype(jnp.bfloat16)


def body(spectra, dead_mask, seg_offsets, src_index):
    ch_count = spectra.shape[0]
    seg_count = spectra.shape[1]
    slice_bins = spectra.shape[3]
    narrow_count = lax.axis_size("narrow")
    wide_count = lax.axis_size("wide")
    total_bins = slice_bins * narrow_count
    narrow_pos = lax.axis_index("narrow")
    wide_pos = lax.axis_index("wide")
    freq_bins = narrow_pos * slice_bins + jnp.arange(slice_bins, dtype=jnp.int32)
    real_part = spectra[:, :, 0].astype(jnp.float32)
    imag_part = spectra[:, :, 1].astype(jnp.float32)
    amplitude = jnp.sqrt(real_part * real_part + imag_part * imag_part)
    padded = padded_2(amplitude, (("narrow", 2),), SMOOTH)
    windowed = window_sums(padded, slice_bins)
    whitened = apply_whitening(
        real_part, imag_part, windowed, freq_bins, total_bins, dead_mask, seg_offsets
    )
    per_block = src_index.shape[0] // wide_count
    own_rows = (
        lax.dynamic_slice_in_dim(src_index, wide_pos * per_block, per_block) - wide_pos * ch_count
    )
    selector = (own_rows[:, None] == jnp.arange(ch_count, dtype=jnp.int32)[None, :]).astype(
        jnp.bfloat16
    )
    chosen = jnp.einsum(
        "rc,ckqf->rkqf", selector, whitened, preferred_element_type=jnp.float32
    ).astype(jnp.bfloat16)
    share_rows = src_index.shape[0] // narrow_count
    norm_factor = 1.0 / math.sqrt(total_bins)
    panel = lax.all_gather(chosen, "wide", axis=0, tiled=True)
    table_part = lag_table(narrow_pos * slice_bins, slice_bins, LAGS)
    block = lax.slice_in_dim(panel, 0, share_rows * lax.axis_size("narrow"), axis=0)
    spectra_x = cross_spectra(whitened, block, seg_count)
    flat = spectra_x.reshape(share_rows * lax.axis_size("narrow") * ch_count, 2 * slice_bins)
    product = jnp.dot(flat, table_part, preferred_element_type=jnp.float32) * norm_factor
    return lax.psum_scatter(
        product.reshape(share_rows * lax.axis_size("narrow"), ch_count, LAGS),
        "narrow",
        scatter_dimension=0,
        tiled=True,
    )


CHUNKS = 4
STEP = 128


def sincos(residue):
    quadrant = (residue + NSAMP // 8) >> (NSAMP // 4).bit_length() - 1
    x = (residue - quadrant * (NSAMP // 4)).astype(jnp.float32) * (2.0 * math.pi / NSAMP)
    y = x * x
    s = x * (1.0 + y * (-1.0 / 6 + y * (1.0 / 120 + y * (-1.0 / 5040 + y * (1.0 / 362880)))))
    c = 1.0 + y * (-0.5 + y * (1.0 / 24 + y * (-1.0 / 720 + y * (1.0 / 40320))))
    odd = (quadrant & 1) == 1
    sine = jnp.where(odd, c, s)
    cosine = jnp.where(odd, s, c)
    sine = jnp.where((quadrant & 2) == 2, -sine, sine)
    cosine = jnp.where(((quadrant + 1) & 2) == 2, -cosine, cosine)
    return cosine, sine


def kernel(
    x_ref, off_ref, dead_ref, pick_ref, o_ref,
    raw, amp, chan, panel, table, rows, ca, sa, cb, sb,
    raw_sem, send, recv,
):
    half = x_ref.shape[1]
    bins = 2 * half
    part = bins // CHUNKS
    lags = o_ref.shape[1]
    w = lax.axis_index("wide")
    n = lax.axis_index("narrow")
    z = w // 4
    x = (w // 2) % 2
    c = w % 2
    rank = z + n * (3 - 2 * z)
    up_z = z + 1 - 2 * n
    down_z = z - 1 + 2 * n

    def device(zv, xv, cv):
        return {"wide": zv * 4 + xv * 2 + cv, "narrow": n}

    up, down = device(up_z, x, c), device(down_z, x, c)
    x_peer, core_peer = device(z, 1 - x, c), device(z, x, 1 - c)
    y_peer = {"wide": w, "narrow": 1 - n}

    def slot(role, xv, cv):
        zl = n if role == 0 else 1 - n
        return zl * 4 + xv * 2 + cv

    barrier = pltpu.get_barrier_semaphore()
    for peer in (y_peer, x_peer, core_peer):
        pl.semaphore_signal(barrier, inc=1, device_id=peer, device_id_type=MESH)

    @pl.when(rank < 3)
    def _():
        pl.semaphore_signal(barrier, inc=1, device_id=up, device_id_type=MESH)

    @pl.when(rank > 0)
    def _():
        pl.semaphore_signal(barrier, inc=1, device_id=down, device_id_type=MESH)

    pl.semaphore_wait(barrier, 3 + (rank + 2) // 3 + (5 - rank) // 3)

    raw_copy = pltpu.make_async_remote_copy(
        src_ref=x_ref,
        dst_ref=raw.at[n],
        send_sem=raw_sem.at[0],
        recv_sem=raw_sem.at[1],
        device_id=y_peer,
        device_id_type=MESH,
    )
    raw_copy.start()
    raw[n] = x_ref[...]

    def lag_steps(count):
        lag = lax.broadcasted_iota(jnp.int32, (count, lags), 1)
        return lag + (NSAMP - lags // 2), lax.broadcasted_iota(jnp.int32, (count, lags), 0)

    steps, at = lag_steps(bins // STEP)
    ca[...], sa[...] = sincos((steps * at * STEP) & (NSAMP - 1))
    steps, at = lag_steps(STEP)
    cb[...], sb[...] = sincos((steps * (at + 1)) & (NSAMP - 1))

    def table_step(a, carry):
        c1 = ca[pl.ds(a, 1), :]
        s1 = sa[pl.ds(a, 1), :]
        for r in range(0, STEP, 16):
            c2 = cb[r : r + 16, :]
            s2 = sb[r : r + 16, :]
            top = pl.ds(pl.multiple_of(a * 2 * STEP + r, 16), 16)
            low = pl.ds(pl.multiple_of(a * 2 * STEP + STEP + r, 16), 16)
            table[top, :] = (c1 * c2 - s1 * s2).astype(jnp.bfloat16)
            table[low, :] = (-s1 * c2 - c1 * s2).astype(jnp.bfloat16)
        return carry

    lax.fori_loop(0, bins // STEP, table_step, 0)

    raw_copy.wait()
    zeros = jnp.zeros((32, STEP), jnp.bfloat16)
    amp[:, 0:STEP] = zeros
    amp[:, STEP + bins : 2 * STEP + bins] = zeros
    for h in range(2):
        re = raw[h, 0:16, :].astype(jnp.float32)
        im = raw[h, 16:32, :].astype(jnp.float32)
        size = jnp.sqrt(re * re + im * im)
        high = size.astype(jnp.bfloat16)
        cols = pl.ds(STEP + h * half, half)
        amp[0:16, cols] = high
        amp[16:32, cols] = (size - high.astype(jnp.float32)).astype(jnp.bfloat16)

    ahead = lax.broadcasted_iota(jnp.int32, (3 * STEP, STEP), 0) - STEP
    ahead = ahead - lax.broadcasted_iota(jnp.int32, (3 * STEP, STEP), 1)
    band = jnp.where(jnp.abs(ahead) <= SMOOTH, 1.0, 0.0).astype(jnp.bfloat16)

    def remote(q, at_slot, kind, target):
        return pltpu.make_async_remote_copy(
            src_ref=panel.at[q, at_slot],
            dst_ref=panel.at[q, at_slot],
            send_sem=send.at[q, kind],
            recv_sem=recv.at[q, at_slot],
            device_id=target,
            device_id_type=MESH,
        )

    def spread(q, role):
        remote(q, slot(role, x, c), 4 + role, x_peer).start()
        remote(q, slot(role, x, c), 6 + role, core_peer).start()

    def arrived(q, at_slot):
        remote(q, at_slot, 0, core_peer).wait_recv()

    def whiten(q):
        blocks = part // STEP
        lhs = jnp.concatenate(
            [amp[:, (q * blocks + b) * STEP : (q * blocks + b + 3) * STEP] for b in range(blocks)],
            axis=0,
        )
        sums = jnp.dot(lhs, band, preferred_element_type=jnp.float32)
        windowed = jnp.concatenate(
            [sums[b * 32 : b * 32 + 16] + sums[b * 32 + 16 : b * 32 + 32] for b in range(blocks)],
            axis=1,
        )
        h, start = q * part // half, q * part % half
        re = raw[h, 0:16, start : start + part].astype(jnp.float32)
        im = raw[h, 16:32, start : start + part].astype(jnp.float32)
        f = lax.broadcasted_iota(jnp.int32, (16, part), 1) + q * part
        counts = jnp.minimum(f + SMOOTH, bins - 1) - jnp.maximum(f - SMOOTH, 0) + 1
        smoothed = windowed / counts.astype(jnp.float32) + EPSILON
        cosine, sine = sincos(((f + 1) * off_ref[:, 0:1]) & (NSAMP - 1))
        scale = dead_ref[:, 0:1] / smoothed
        white = jnp.concatenate(
            [
                ((re * cosine - im * sine) * scale).astype(jnp.bfloat16),
                ((re * sine + im * cosine) * scale).astype(jnp.bfloat16),
            ],
            axis=0,
        )
        picked = jnp.dot(pick_ref[...], white, preferred_element_type=jnp.float32)
        chan[q] = picked[16:]
        mine = picked[0:16].astype(jnp.bfloat16)

        @pl.when(rank == 0)
        def _():
            panel[q, slot(0, x, c)] = mine
            remote(q, slot(0, x, c), 0, up).start()
            spread(q, 0)

        @pl.when(rank == 1)
        def _():
            panel[q, slot(1, x, c)] = mine
            remote(q, slot(1, x, c), 0, up).start()
            remote(q, slot(1, x, c), 1, down).start()
            spread(q, 1)

    def along_z(q):
        @pl.when(rank > 0)
        def _():
            arrived(q, slot(0, x, c))

            @pl.when(rank < 3)
            def _():
                remote(q, slot(0, x, c), 2, up).start()

            spread(q, 0)

        @pl.when(rank != 1)
        def _():
            arrived(q, slot(1, x, c))

            @pl.when(rank == 2)
            def _():
                remote(q, slot(1, x, c), 3, up).start()

            spread(q, 1)

    def along_x(q):
        for role in range(2):
            arrived(q, slot(role, 1 - x, c))
            remote(q, slot(role, 1 - x, c), 8 + role, core_peer).start()

    def correlate(q):
        for role in range(2):
            for xv in range(2):
                arrived(q, slot(role, xv, 1 - c))
        first = lax.broadcasted_iota(jnp.int32, (8, STEP), 0) < 4
        norm = 1.0 / math.sqrt(2)

        def cross(a, carry):
            lanes = pl.ds(pl.multiple_of(a * STEP, STEP), STEP)
            source = [panel[q, b, :, lanes].astype(jnp.float32) for b in range(8)]
            for ch in range(6):
                own = chan[q, ch * 16 : ch * 16 + 16, lanes]
                cr, ci = own[0:8], own[8:16]
                for imag in range(2):
                    terms = []
                    for b in range(8):
                        sr, si = source[b][0:8], source[b][8:16]
                        terms.append(sr * ci - si * cr if imag else sr * cr + si * ci)
                    pairs = []
                    for b in range(0, 8, 2):
                        keep = jnp.where(first, terms[b], terms[b + 1])
                        move = jnp.where(first, terms[b + 1], terms[b])
                        pairs.append(keep + pltpu.roll(move, 4, 0))
                    joined = jnp.concatenate(pairs, axis=0) * norm
                    cols = pl.ds(pl.multiple_of((2 * a + imag) * STEP, STEP), STEP)
                    rows[ch * 32 : ch * 32 + 32, cols] = joined.astype(jnp.bfloat16)
            return carry

        lax.fori_loop(0, part // STEP, cross, 0)
        product = jnp.dot(
            rows[...],
            table[q * 2 * part : (q + 1) * 2 * part, :],
            preferred_element_type=jnp.float32,
        ) * (1.0 / math.sqrt(bins))
        if q == 0:
            o_ref[...] = product
        else:
            o_ref[...] += product

    for q in range(CHUNKS):
        whiten(q)
    for t in range(CHUNKS + 2):
        if t < CHUNKS:
            along_z(t)
        if 0 <= t - 1 < CHUNKS:
            along_x(t - 1)
        if 0 <= t - 2:
            correlate(t - 2)

    for q in range(CHUNKS):
        @pl.when(rank < 2)
        def _():
            remote(q, 0, 0, core_peer).wait_send()

        @pl.when(rank == 1)
        def _():
            remote(q, 0, 1, core_peer).wait_send()

        @pl.when((rank + 1) // 2 == 1)
        def _():
            remote(q, 0, 2, core_peer).wait_send()

        @pl.when(rank == 2)
        def _():
            remote(q, 0, 3, core_peer).wait_send()

        for kind in range(4, 10):
            remote(q, 0, kind, core_peer).wait_send()


def fused_body(spectra, dead_mask, seg_offsets, src_index):
    ch_count, seg_count, _, half = spectra.shape
    bins = 2 * half
    wide_pos = lax.axis_index("wide")
    spare = 8 - ch_count
    cells = jnp.pad(spectra.transpose(2, 1, 0, 3), ((0, 0), (0, 0), (0, spare), (0, 0)))
    cells = cells.reshape(32, half)
    off = jnp.pad(seg_offsets.T, ((0, 0), (0, spare))).reshape(16, 1)
    dead = jnp.pad(dead_mask.astype(jnp.float32), (0, spare))
    dead = jnp.concatenate([dead, dead]).reshape(16, 1)
    own = lax.dynamic_slice_in_dim(src_index, wide_pos * 4, 4) - wide_pos * ch_count
    plane = jnp.arange(4, dtype=jnp.int32) * 8
    head = (plane[:, None] + own[None, :]).reshape(16)
    tail = jnp.arange(ch_count, dtype=jnp.int32)[:, None, None] + plane[None, :, None]
    tail = jnp.broadcast_to(tail, (ch_count, 4, 4)).reshape(ch_count * 16)
    wanted = jnp.concatenate([head, tail])
    pick = (wanted[:, None] == jnp.arange(32, dtype=jnp.int32)[None, :]).astype(jnp.bfloat16)
    shares = src_index.shape[0] // 2
    vmem = pl.BlockSpec(memory_space=pltpu.VMEM)
    f32, bf16 = jnp.float32, jnp.bfloat16
    result = pl.pallas_call(
        kernel,
        out_shape=jax.ShapeDtypeStruct((ch_count * shares, LAGS), f32),
        in_specs=[vmem] * 4,
        out_specs=vmem,
        scratch_shapes=[
            pltpu.VMEM((2, 32, half), bf16),
            pltpu.VMEM((32, bins + 2 * STEP), bf16),
            pltpu.VMEM((CHUNKS, ch_count * 16, bins // CHUNKS), f32),
            pltpu.VMEM((CHUNKS, 8, 16, bins // CHUNKS), bf16),
            pltpu.VMEM((2 * bins, LAGS), bf16),
            pltpu.VMEM((ch_count * shares, 2 * bins // CHUNKS), bf16),
            pltpu.VMEM((bins // STEP, LAGS), f32),
            pltpu.VMEM((bins // STEP, LAGS), f32),
            pltpu.VMEM((STEP, LAGS), f32),
            pltpu.VMEM((STEP, LAGS), f32),
            pltpu.SemaphoreType.DMA((2,)),
            pltpu.SemaphoreType.DMA((CHUNKS, 10)),
            pltpu.SemaphoreType.DMA((CHUNKS, 8)),
        ],
        compiler_params=pltpu.CompilerParams(
            collective_id=0, has_side_effects=True, vmem_limit_bytes=40 * 1024 * 1024
        ),
    )(
        cells,
        jnp.broadcast_to(off, (16, STEP)),
        jnp.broadcast_to(dead, (16, STEP)),
        pick,
    )
    return result.reshape(ch_count, shares, LAGS).transpose(1, 0, 2)


def solution(mesh):
    placed = (P("wide", None, None, "narrow"), P("wide"), P("wide", None), P())
    fits = mesh.shape["wide"] == 16 and mesh.shape["narrow"] == 2
    return jax.shard_map(
        fused_body if fits else body,
        mesh=mesh,
        in_specs=placed,
        out_specs=P("narrow", "wide", None),
        check_vma=False,
    )
```

```python
import math

import jax
import jax.numpy as jnp
from jax import lax
from jax.experimental import pallas as pl
from jax.experimental.pallas import tpu as pltpu
from jax.sharding import PartitionSpec as P

NSAMP = 32768
LAGS = 512
SMOOTH = 64


EPSILON = 1e-06
MESH = pl.DeviceIdType.MESH


def padded_2(cells, sides, width):
    for axis, dim in sides:
        count = lax.axis_size(axis)
        ends = count - 1
        head = lax.slice_in_dim(cells, 0, width, axis=dim)
        tail = lax.slice_in_dim(cells, cells.shape[dim] - width, cells.shape[dim], axis=dim)
        cells = jnp.concatenate(
            [
                lax.ppermute(tail, axis, [(i, (i + 1) % count) for i in range(ends)]),
                cells,
                lax.ppermute(head, axis, [((i + 1) % count, i) for i in range(ends)]),
            ],
            axis=dim,
        )
    return cells


def window_sums(padded, bins):
    step = 2 * SMOOTH
    blocks = bins // step
    head = padded[..., :bins].reshape(padded.shape[:-1] + (blocks, step))
    tail = padded[..., step:].reshape(padded.shape[:-1] + (blocks, step))
    cells = jnp.concatenate([head, tail], axis=-1)
    ahead = jnp.arange(2 * step)[:, None] - jnp.arange(step)[None, :]
    band = ((ahead >= 0) & (ahead <= step)).astype(jnp.float32)
    sums = jnp.einsum("ckbi,io->ckbo", cells, band, precision=lax.Precision.HIGHEST)
    return sums.reshape(padded.shape[:-1] + (bins,))


def turns(product):
    angles = 2.0 * math.pi / NSAMP * (product % NSAMP).astype(jnp.float32)
    return jnp.cos(angles), jnp.sin(angles)


def lag_table(first, length, lag_count):
    step = 128
    lag_steps = jnp.arange(lag_count, dtype=jnp.int32) - lag_count // 2 + NSAMP
    coarse = first + step * jnp.arange(length // step, dtype=jnp.int32)
    fine = jnp.arange(step, dtype=jnp.int32) + 1
    ca, sa = turns(coarse[:, None] * lag_steps[None, :])
    cb, sb = turns(fine[:, None] * lag_steps[None, :])
    cosine = ca[:, None] * cb[None] - sa[:, None] * sb[None]
    sine = sa[:, None] * cb[None] + ca[:, None] * sb[None]
    return jnp.concatenate(
        [cosine.reshape(length, lag_count), -sine.reshape(length, lag_count)], axis=0
    ).astype(jnp.bfloat16)


def apply_whitening(real_part, imag_part, windowed, freq_bins, total_bins, dead_mask, seg_offsets):
    counts = (
        jnp.minimum(freq_bins + SMOOTH, total_bins - 1) - jnp.maximum(freq_bins - SMOOTH, 0) + 1
    ).astype(jnp.float32)
    smoothed = windowed / counts + EPSILON
    residue = (freq_bins + 1)[None, None, :] * seg_offsets[:, :, None] % NSAMP
    phase = 2.0 * math.pi / NSAMP * residue.astype(jnp.float32)
    scale = dead_mask.astype(jnp.float32)[:, None, None] / smoothed
    cosine = jnp.cos(phase)
    sine = jnp.sin(phase)
    white_real = (real_part * cosine - imag_part * sine) * scale
    white_imag = (real_part * sine + imag_part * cosine) * scale
    return jnp.stack([white_real, white_imag], axis=2).astype(jnp.bfloat16)


def cross_spectra(channels, sources, seg_count):
    chan_real = channels[:, :, 0]
    chan_imag = channels[:, :, 1]
    src_real = sources[:, :, 0]
    src_imag = sources[:, :, 1]
    cross_real = jnp.einsum(
        "ckf,skf->scf", chan_real, src_real, preferred_element_type=jnp.float32
    ) + jnp.einsum("ckf,skf->scf", chan_imag, src_imag, preferred_element_type=jnp.float32)
    cross_imag = jnp.einsum(
        "ckf,skf->scf", chan_imag, src_real, preferred_element_type=jnp.float32
    ) - jnp.einsum("ckf,skf->scf", chan_real, src_imag, preferred_element_type=jnp.float32)
    joined = jnp.concatenate([cross_real, cross_imag], axis=-1) * (1.0 / math.sqrt(seg_count))
    return joined.astype(jnp.bfloat16)


def body(spectra, dead_mask, seg_offsets, src_index):
    ch_count = spectra.shape[0]
    seg_count = spectra.shape[1]
    slice_bins = spectra.shape[3]
    narrow_count = lax.axis_size("narrow")
    wide_count = lax.axis_size("wide")
    total_bins = slice_bins * narrow_count
    narrow_pos = lax.axis_index("narrow")
    wide_pos = lax.axis_index("wide")
    freq_bins = narrow_pos * slice_bins + jnp.arange(slice_bins, dtype=jnp.int32)
    real_part = spectra[:, :, 0].astype(jnp.float32)
    imag_part = spectra[:, :, 1].astype(jnp.float32)
    amplitude = jnp.sqrt(real_part * real_part + imag_part * imag_part)
    padded = padded_2(amplitude, (("narrow", 2),), SMOOTH)
    windowed = window_sums(padded, slice_bins)
    whitened = apply_whitening(
        real_part, imag_part, windowed, freq_bins, total_bins, dead_mask, seg_offsets
    )
    per_block = src_index.shape[0] // wide_count
    own_rows = (
        lax.dynamic_slice_in_dim(src_index, wide_pos * per_block, per_block) - wide_pos * ch_count
    )
    selector = (own_rows[:, None] == jnp.arange(ch_count, dtype=jnp.int32)[None, :]).astype(
        jnp.bfloat16
    )
    chosen = jnp.einsum(
        "rc,ckqf->rkqf", selector, whitened, preferred_element_type=jnp.float32
    ).astype(jnp.bfloat16)
    share_rows = src_index.shape[0] // narrow_count
    norm_factor = 1.0 / math.sqrt(total_bins)
    panel = lax.all_gather(chosen, "wide", axis=0, tiled=True)
    table_part = lag_table(narrow_pos * slice_bins, slice_bins, LAGS)
    block = lax.slice_in_dim(panel, 0, share_rows * lax.axis_size("narrow"), axis=0)
    spectra_x = cross_spectra(whitened, block, seg_count)
    flat = spectra_x.reshape(share_rows * lax.axis_size("narrow") * ch_count, 2 * slice_bins)
    product = jnp.dot(flat, table_part, preferred_element_type=jnp.float32) * norm_factor
    return lax.psum_scatter(
        product.reshape(share_rows * lax.axis_size("narrow"), ch_count, LAGS),
        "narrow",
        scatter_dimension=0,
        tiled=True,
    )


CHUNKS = 4
STEP = 128


def sincos(residue):
    quadrant = (residue + NSAMP // 8) >> (NSAMP // 4).bit_length() - 1
    x = (residue - quadrant * (NSAMP // 4)).astype(jnp.float32) * (2.0 * math.pi / NSAMP)
    y = x * x
    s = x * (1.0 + y * (-1.0 / 6 + y * (1.0 / 120 + y * (-1.0 / 5040 + y * (1.0 / 362880)))))
    c = 1.0 + y * (-0.5 + y * (1.0 / 24 + y * (-1.0 / 720 + y * (1.0 / 40320))))
    odd = (quadrant & 1) == 1
    sine = jnp.where(odd, c, s)
    cosine = jnp.where(odd, s, c)
    sine = jnp.where((quadrant & 2) == 2, -sine, sine)
    cosine = jnp.where(((quadrant + 1) & 2) == 2, -cosine, cosine)
    return cosine, sine


def kernel(
    x_ref, off_ref, dead_ref, src_ref, o_ref,
    amp, halo, white, chan, panel, relay, table, rows, ca, sa, cb, sb,
    halo_sem, send, recv, relay_recv, white_recv,
):
    half = x_ref.shape[1]
    bins = 2 * half
    part = bins // CHUNKS
    lags = o_ref.shape[1]
    w = lax.axis_index("wide")
    n = lax.axis_index("narrow")
    z = w // 4
    x = (w // 2) % 2
    c = w % 2
    rank = z + n * (3 - 2 * z)
    up_z = z + 1 - 2 * n
    down_z = z - 1 + 2 * n

    def device(zv, xv, cv):
        return {"wide": zv * 4 + xv * 2 + cv, "narrow": n}

    up, down = device(up_z, x, c), device(down_z, x, c)
    x_peer, core_peer = device(z, 1 - x, c), device(z, x, 1 - c)
    y_peer = {"wide": w, "narrow": 1 - n}

    def slot(role, xv, cv):
        return (n if role == 0 else 1 - n) * 4 + xv * 2 + cv

    def peer_slot(role):
        return (1 - n if role == 0 else n) * 4 + x * 2 + c

    def chunk(q):
        return q + n * (3 - 2 * q)

    barrier = pltpu.get_barrier_semaphore()
    for peer in (y_peer, x_peer, core_peer):
        pl.semaphore_signal(barrier, inc=1, device_id=peer, device_id_type=MESH)

    @pl.when(rank < 3)
    def _():
        pl.semaphore_signal(barrier, inc=1, device_id=up, device_id_type=MESH)

    @pl.when(rank > 0)
    def _():
        pl.semaphore_signal(barrier, inc=1, device_id=down, device_id_type=MESH)

    def amplitude(cells):
        re = cells[0:16].astype(jnp.float32)
        im = cells[16:32].astype(jnp.float32)
        size = jnp.sqrt(re * re + im * im)
        high = size.astype(jnp.bfloat16)
        return high, (size - high.astype(jnp.float32)).astype(jnp.bfloat16)

    zeros = jnp.zeros((32, STEP), jnp.bfloat16)
    amp[:, 0:STEP] = zeros
    amp[:, STEP + half : 2 * STEP + half] = zeros
    high, low = amplitude(x_ref[...])
    amp[0:16, STEP : STEP + half] = high
    amp[16:32, STEP : STEP + half] = low

    ahead = lax.broadcasted_iota(jnp.int32, (3 * STEP, STEP), 0) - STEP
    ahead = ahead - lax.broadcasted_iota(jnp.int32, (3 * STEP, STEP), 1)
    band = jnp.where(jnp.abs(ahead) <= SMOOTH, 1.0, 0.0).astype(jnp.bfloat16)

    line = lax.broadcasted_iota(jnp.int32, (16, STEP), 0)
    offsets = jnp.zeros((16, STEP), jnp.int32)
    live = jnp.zeros((16, STEP), jnp.int32)
    for ch in range(6):
        live = jnp.where((line & 7) == ch, dead_ref[ch], live)
        for k in range(2):
            offsets = jnp.where(line == k * 8 + ch, off_ref[k, ch], offsets)
    offsets = offsets[:, 0:1]
    live = live[:, 0:1].astype(jnp.float32)
    line = lax.broadcasted_iota(jnp.int32, (112, 32), 0)
    wanted = (line >> 4) - 1
    for r in range(4):
        wanted = jnp.where((line & 3) + (line >> 4) * 4 == r, src_ref[w * 4 + r] - w * 6, wanted)
    wanted = wanted + ((line & 15) >> 2) * 8
    column = lax.broadcasted_iota(jnp.int32, (112, 32), 1)
    pick = jnp.where(wanted == column, 1.0, 0.0).astype(jnp.bfloat16)

    pl.semaphore_wait(barrier, 3 + (rank + 2) // 3 + (5 - rank) // 3)

    edge = pl.ds(pl.multiple_of((1 - n) * (half - STEP), STEP), STEP)
    halo_copy = pltpu.make_async_remote_copy(
        src_ref=x_ref.at[:, edge],
        dst_ref=halo,
        send_sem=halo_sem.at[0],
        recv_sem=halo_sem.at[1],
        device_id=y_peer,
        device_id_type=MESH,
    )
    halo_copy.start()

    def remote(q, at_slot, kind, target):
        return pltpu.make_async_remote_copy(
            src_ref=panel.at[chunk(q), at_slot],
            dst_ref=panel.at[chunk(q), at_slot],
            send_sem=send.at[q, kind],
            recv_sem=recv.at[chunk(q), at_slot],
            device_id=target,
            device_id_type=MESH,
        )

    def relayed(q, role):
        return pltpu.make_async_remote_copy(
            src_ref=relay.at[q, role],
            dst_ref=relay.at[q, role],
            send_sem=send.at[q, 10 + role],
            recv_sem=relay_recv.at[q, role],
            device_id=down,
            device_id_type=MESH,
        )

    def crossing(q, role):
        return pltpu.make_async_remote_copy(
            src_ref=relay.at[q, role],
            dst_ref=panel.at[chunk(q), peer_slot(role)],
            send_sem=send.at[q, 12 + role],
            recv_sem=recv.at[chunk(q), peer_slot(role)],
            device_id=y_peer,
            device_id_type=MESH,
        )

    def white_copy(q, g):
        return pltpu.make_async_remote_copy(
            src_ref=white.at[g],
            dst_ref=white.at[g],
            send_sem=send.at[q, 14],
            recv_sem=white_recv.at[g],
            device_id=y_peer,
            device_id_type=MESH,
        )

    def spread(q, role):
        remote(q, slot(role, x, c), 4 + role, x_peer).start()
        remote(q, slot(role, x, c), 6 + role, core_peer).start()

    def arrived(q, at_slot):
        remote(q, at_slot, 0, core_peer).wait_recv()

    def choose(q, cells):
        picked = jnp.dot(pick, cells, preferred_element_type=jnp.float32)
        chan[chunk(q)] = picked[16:]
        return picked[0:16].astype(jnp.bfloat16)

    def whiten(q):
        blocks = part // STEP
        g = chunk(q)
        start = (g - 2 * n) * part
        lhs = jnp.concatenate(
            [
                amp[:, pl.ds(pl.multiple_of(start + b * STEP, STEP), 3 * STEP)]
                for b in range(blocks)
            ],
            axis=0,
        )
        sums = jnp.dot(lhs, band, preferred_element_type=jnp.float32)
        windowed = jnp.concatenate(
            [sums[b * 32 : b * 32 + 16] + sums[b * 32 + 16 : b * 32 + 32] for b in range(blocks)],
            axis=1,
        )
        lanes = pl.ds(pl.multiple_of(start, STEP), part)
        re = x_ref[0:16, lanes].astype(jnp.float32)
        im = x_ref[16:32, lanes].astype(jnp.float32)
        f = lax.broadcasted_iota(jnp.int32, (16, part), 1) + g * part
        counts = jnp.minimum(f + SMOOTH, bins - 1) - jnp.maximum(f - SMOOTH, 0) + 1
        smoothed = windowed / counts.astype(jnp.float32) + EPSILON
        cosine, sine = sincos(((f + 1) * offsets) & (NSAMP - 1))
        scale = live / smoothed
        cells = jnp.concatenate(
            [
                ((re * cosine - im * sine) * scale).astype(jnp.bfloat16),
                ((re * sine + im * cosine) * scale).astype(jnp.bfloat16),
            ],
            axis=0,
        )
        white[g] = cells
        mine = choose(q, cells)

        @pl.when(rank == 0)
        def _():
            panel[g, slot(0, x, c)] = mine
            remote(q, slot(0, x, c), 0, up).start()
            spread(q, 0)

        @pl.when(rank == 1)
        def _():
            panel[g, slot(1, x, c)] = mine
            remote(q, slot(1, x, c), 0, up).start()
            remote(q, slot(1, x, c), 1, down).start()
            spread(q, 1)

        @pl.when(rank == 2)
        def _():
            relay[q, 1] = mine
            relayed(q, 1).start()

        @pl.when(rank == 3)
        def _():
            relay[q, 0] = mine
            relayed(q, 0).start()

        white_copy(q, g).start()

    def along_z(q):
        @pl.when(rank == 0)
        def _():
            arrived(q, slot(1, x, c))
            spread(q, 1)
            for role in range(2):
                relayed(q, role).wait_recv()
                crossing(q, role).start()

        @pl.when(rank == 1)
        def _():
            arrived(q, slot(0, x, c))
            remote(q, slot(0, x, c), 2, up).start()
            spread(q, 0)
            for role in (1, 0):
                relayed(q, role).wait_recv()
                relayed(q, role).start()
                crossing(q, role).start()

        @pl.when(rank == 2)
        def _():
            relayed(q, 0).wait_recv()
            relayed(q, 0).start()
            for role in (1, 0):
                arrived(q, slot(role, x, c))
                remote(q, slot(role, x, c), 2 + role, up).start()
                spread(q, role)

        @pl.when(rank == 3)
        def _():
            for role in (1, 0):
                arrived(q, slot(role, x, c))
                spread(q, role)

    def along_y(q):
        g = chunk(q)
        white_copy(q, g).wait_recv()
        mine = choose(q, white[g])

        @pl.when(rank == 0)
        def _():
            panel[g, slot(0, x, c)] = mine
            remote(q, slot(0, x, c), 0, up).start()
            spread(q, 0)

        @pl.when(rank == 1)
        def _():
            panel[g, slot(1, x, c)] = mine
            remote(q, slot(1, x, c), 1, down).start()
            spread(q, 1)

    def after_y(q):
        @pl.when(rank == 0)
        def _():
            arrived(q, slot(1, x, c))
            spread(q, 1)

        @pl.when(rank == 1)
        def _():
            arrived(q, slot(0, x, c))
            spread(q, 0)

        @pl.when(rank > 1)
        def _():
            for role in (1, 0):
                arrived(q, slot(role, x, c))
                spread(q, role)

    def along_x(q):
        for role in range(2):
            arrived(q, slot(role, 1 - x, c))
            remote(q, slot(role, 1 - x, c), 8 + role, core_peer).start()

    def lag_steps(count):
        lag = lax.broadcasted_iota(jnp.int32, (count, lags), 1)
        return lag + (NSAMP - lags // 2), lax.broadcasted_iota(jnp.int32, (count, lags), 0)

    def table_base():
        steps, at = lag_steps(bins // STEP)
        ca[...], sa[...] = sincos((steps * at * STEP) & (NSAMP - 1))
        steps, at = lag_steps(STEP)
        cb[...], sb[...] = sincos((steps * (at + 1)) & (NSAMP - 1))

    def table_part(q):
        first = chunk(q) * (part // STEP)

        def table_step(i, carry):
            a = first + i
            c1 = ca[pl.ds(a, 1), :]
            s1 = sa[pl.ds(a, 1), :]
            for r in range(0, STEP, 16):
                c2 = cb[r : r + 16, :]
                s2 = sb[r : r + 16, :]
                top = pl.ds(pl.multiple_of(a * 2 * STEP + r, 16), 16)
                low = pl.ds(pl.multiple_of(a * 2 * STEP + STEP + r, 16), 16)
                table[top, :] = (c1 * c2 - s1 * s2).astype(jnp.bfloat16)
                table[low, :] = (-s1 * c2 - c1 * s2).astype(jnp.bfloat16)
            return carry

        lax.fori_loop(0, part // STEP, table_step, 0)

    def correlate(q):
        for role in range(2):
            for xv in range(2):
                arrived(q, slot(role, xv, 1 - c))
        g = chunk(q)
        first = lax.broadcasted_iota(jnp.int32, (8, STEP), 0) < 4
        norm = 1.0 / math.sqrt(2)

        def cross(a, carry):
            lanes = pl.ds(pl.multiple_of(a * STEP, STEP), STEP)
            source = [panel[g, b, :, lanes].astype(jnp.float32) for b in range(8)]
            for ch in range(6):
                own = chan[g, ch * 16 : ch * 16 + 16, lanes]
                cr, ci = own[0:8], own[8:16]
                for imag in range(2):
                    terms = []
                    for b in range(8):
                        sr, si = source[b][0:8], source[b][8:16]
                        terms.append(sr * ci - si * cr if imag else sr * cr + si * ci)
                    pairs = []
                    for b in range(0, 8, 2):
                        keep = jnp.where(first, terms[b], terms[b + 1])
                        move = jnp.where(first, terms[b + 1], terms[b])
                        pairs.append(keep + pltpu.roll(move, 4, 0))
                    joined = jnp.concatenate(pairs, axis=0) * norm
                    cols = pl.ds(pl.multiple_of((2 * a + imag) * STEP, STEP), STEP)
                    rows[ch * 32 : ch * 32 + 32, cols] = joined.astype(jnp.bfloat16)
            return carry

        lax.fori_loop(0, part // STEP, cross, 0)
        product = jnp.dot(
            rows[...],
            table[pl.ds(pl.multiple_of(g * 2 * part, 16), 2 * part), :],
            preferred_element_type=jnp.float32,
        ) * (1.0 / math.sqrt(bins))
        if q == 0:
            o_ref[...] = product
        else:
            o_ref[...] += product

    whiten(0)
    table_base()
    halo_copy.wait()
    high, low = amplitude(halo[...])
    edge = pl.ds(pl.multiple_of((1 - n) * (half + STEP), STEP), STEP)
    amp[0:16, edge] = high
    amp[16:32, edge] = low
    whiten(1)
    along_z(0)
    table_part(0)
    along_z(1)
    along_y(3)
    along_x(0)
    table_part(1)
    along_y(2)
    after_y(3)
    along_x(1)
    correlate(0)
    after_y(2)
    along_x(3)
    table_part(3)
    correlate(1)
    along_x(2)
    table_part(2)
    correlate(3)
    correlate(2)

    def sent(q, kind):
        remote(q, 0, kind, core_peer).wait_send()

    for q in range(CHUNKS):
        own_half = q < 2

        @pl.when(rank == 0)
        def _():
            for kind in (0, 12, 13) if own_half else (0,):
                sent(q, kind)

        @pl.when(rank == 1)
        def _():
            for kind in (0, 1, 2, 10, 11, 12, 13) if own_half else (1,):
                sent(q, kind)

        if own_half:
            white_copy(q, chunk(q)).wait_send()

            @pl.when(rank == 2)
            def _():
                for kind in (2, 3, 10, 11):
                    sent(q, kind)

            @pl.when(rank == 3)
            def _():
                sent(q, 10)

        for kind in range(4, 10):
            sent(q, kind)


def fused_body(spectra, dead_mask, seg_offsets, src_index):
    ch_count, seg_count, _, half = spectra.shape
    bins = 2 * half
    part = bins // CHUNKS
    spare = 8 - ch_count
    cells = jnp.pad(spectra.transpose(2, 1, 0, 3), ((0, 0), (0, 0), (0, spare), (0, 0)))
    cells = cells.reshape(32, half)
    shares = src_index.shape[0] // 2
    vmem = pl.BlockSpec(memory_space=pltpu.VMEM)
    smem = pl.BlockSpec(memory_space=pltpu.SMEM)
    f32, bf16 = jnp.float32, jnp.bfloat16
    result = pl.pallas_call(
        kernel,
        out_shape=jax.ShapeDtypeStruct((ch_count * shares, LAGS), f32),
        in_specs=[vmem, smem, smem, smem],
        out_specs=vmem,
        scratch_shapes=[
            pltpu.VMEM((32, half + 2 * STEP), bf16),
            pltpu.VMEM((32, STEP), bf16),
            pltpu.VMEM((CHUNKS, 32, part), bf16),
            pltpu.VMEM((CHUNKS, ch_count * 16, part), f32),
            pltpu.VMEM((CHUNKS, 8, 16, part), bf16),
            pltpu.VMEM((2, 2, 16, part), bf16),
            pltpu.VMEM((2 * bins, LAGS), bf16),
            pltpu.VMEM((ch_count * shares, 2 * part), bf16),
            pltpu.VMEM((bins // STEP, LAGS), f32),
            pltpu.VMEM((bins // STEP, LAGS), f32),
            pltpu.VMEM((STEP, LAGS), f32),
            pltpu.VMEM((STEP, LAGS), f32),
            pltpu.SemaphoreType.DMA((2,)),
            pltpu.SemaphoreType.DMA((CHUNKS, 15)),
            pltpu.SemaphoreType.DMA((CHUNKS, 8)),
            pltpu.SemaphoreType.DMA((2, 2)),
            pltpu.SemaphoreType.DMA((CHUNKS,)),
        ],
        compiler_params=pltpu.CompilerParams(
            collective_id=0, has_side_effects=True, vmem_limit_bytes=40 * 1024 * 1024
        ),
    )(cells, seg_offsets.T, dead_mask, src_index)
    return result.reshape(ch_count, shares, LAGS).transpose(1, 0, 2)


def solution(mesh):
    placed = (P("wide", None, None, "narrow"), P("wide"), P("wide", None), P())
    fits = mesh.shape["wide"] == 16 and mesh.shape["narrow"] == 2
    return jax.shard_map(
        fused_body if fits else body,
        mesh=mesh,
        in_specs=placed,
        out_specs=P("narrow", "wide", None),
        check_vma=False,
    )
```

```python
import math

import jax
import jax.numpy as jnp
from jax import lax
from jax.experimental import pallas as pl
from jax.experimental.pallas import tpu as pltpu
from jax.sharding import PartitionSpec as P

NSAMP = 32768
LAGS = 512
SMOOTH = 64


EPSILON = 1e-06
MESH = pl.DeviceIdType.MESH


def padded_2(cells, sides, width):
    for axis, dim in sides:
        count = lax.axis_size(axis)
        ends = count - 1
        head = lax.slice_in_dim(cells, 0, width, axis=dim)
        tail = lax.slice_in_dim(cells, cells.shape[dim] - width, cells.shape[dim], axis=dim)
        cells = jnp.concatenate(
            [
                lax.ppermute(tail, axis, [(i, (i + 1) % count) for i in range(ends)]),
                cells,
                lax.ppermute(head, axis, [((i + 1) % count, i) for i in range(ends)]),
            ],
            axis=dim,
        )
    return cells


def window_sums(padded, bins):
    step = 2 * SMOOTH
    blocks = bins // step
    head = padded[..., :bins].reshape(padded.shape[:-1] + (blocks, step))
    tail = padded[..., step:].reshape(padded.shape[:-1] + (blocks, step))
    cells = jnp.concatenate([head, tail], axis=-1)
    ahead = jnp.arange(2 * step)[:, None] - jnp.arange(step)[None, :]
    band = ((ahead >= 0) & (ahead <= step)).astype(jnp.float32)
    sums = jnp.einsum("ckbi,io->ckbo", cells, band, precision=lax.Precision.HIGHEST)
    return sums.reshape(padded.shape[:-1] + (bins,))


def turns(product):
    angles = 2.0 * math.pi / NSAMP * (product % NSAMP).astype(jnp.float32)
    return jnp.cos(angles), jnp.sin(angles)


def lag_table(first, length, lag_count):
    step = 128
    lag_steps = jnp.arange(lag_count, dtype=jnp.int32) - lag_count // 2 + NSAMP
    coarse = first + step * jnp.arange(length // step, dtype=jnp.int32)
    fine = jnp.arange(step, dtype=jnp.int32) + 1
    ca, sa = turns(coarse[:, None] * lag_steps[None, :])
    cb, sb = turns(fine[:, None] * lag_steps[None, :])
    cosine = ca[:, None] * cb[None] - sa[:, None] * sb[None]
    sine = sa[:, None] * cb[None] + ca[:, None] * sb[None]
    return jnp.concatenate(
        [cosine.reshape(length, lag_count), -sine.reshape(length, lag_count)], axis=0
    ).astype(jnp.bfloat16)


def apply_whitening(real_part, imag_part, windowed, freq_bins, total_bins, dead_mask, seg_offsets):
    counts = (
        jnp.minimum(freq_bins + SMOOTH, total_bins - 1) - jnp.maximum(freq_bins - SMOOTH, 0) + 1
    ).astype(jnp.float32)
    smoothed = windowed / counts + EPSILON
    residue = (freq_bins + 1)[None, None, :] * seg_offsets[:, :, None] % NSAMP
    phase = 2.0 * math.pi / NSAMP * residue.astype(jnp.float32)
    scale = dead_mask.astype(jnp.float32)[:, None, None] / smoothed
    cosine = jnp.cos(phase)
    sine = jnp.sin(phase)
    white_real = (real_part * cosine - imag_part * sine) * scale
    white_imag = (real_part * sine + imag_part * cosine) * scale
    return jnp.stack([white_real, white_imag], axis=2).astype(jnp.bfloat16)


def cross_spectra(channels, sources, seg_count):
    chan_real = channels[:, :, 0]
    chan_imag = channels[:, :, 1]
    src_real = sources[:, :, 0]
    src_imag = sources[:, :, 1]
    cross_real = jnp.einsum(
        "ckf,skf->scf", chan_real, src_real, preferred_element_type=jnp.float32
    ) + jnp.einsum("ckf,skf->scf", chan_imag, src_imag, preferred_element_type=jnp.float32)
    cross_imag = jnp.einsum(
        "ckf,skf->scf", chan_imag, src_real, preferred_element_type=jnp.float32
    ) - jnp.einsum("ckf,skf->scf", chan_real, src_imag, preferred_element_type=jnp.float32)
    joined = jnp.concatenate([cross_real, cross_imag], axis=-1) * (1.0 / math.sqrt(seg_count))
    return joined.astype(jnp.bfloat16)


def body(spectra, dead_mask, seg_offsets, src_index):
    ch_count = spectra.shape[0]
    seg_count = spectra.shape[1]
    slice_bins = spectra.shape[3]
    narrow_count = lax.axis_size("narrow")
    wide_count = lax.axis_size("wide")
    total_bins = slice_bins * narrow_count
    narrow_pos = lax.axis_index("narrow")
    wide_pos = lax.axis_index("wide")
    freq_bins = narrow_pos * slice_bins + jnp.arange(slice_bins, dtype=jnp.int32)
    real_part = spectra[:, :, 0].astype(jnp.float32)
    imag_part = spectra[:, :, 1].astype(jnp.float32)
    amplitude = jnp.sqrt(real_part * real_part + imag_part * imag_part)
    padded = padded_2(amplitude, (("narrow", 2),), SMOOTH)
    windowed = window_sums(padded, slice_bins)
    whitened = apply_whitening(
        real_part, imag_part, windowed, freq_bins, total_bins, dead_mask, seg_offsets
    )
    per_block = src_index.shape[0] // wide_count
    own_rows = (
        lax.dynamic_slice_in_dim(src_index, wide_pos * per_block, per_block) - wide_pos * ch_count
    )
    selector = (own_rows[:, None] == jnp.arange(ch_count, dtype=jnp.int32)[None, :]).astype(
        jnp.bfloat16
    )
    chosen = jnp.einsum(
        "rc,ckqf->rkqf", selector, whitened, preferred_element_type=jnp.float32
    ).astype(jnp.bfloat16)
    share_rows = src_index.shape[0] // narrow_count
    norm_factor = 1.0 / math.sqrt(total_bins)
    panel = lax.all_gather(chosen, "wide", axis=0, tiled=True)
    table_part = lag_table(narrow_pos * slice_bins, slice_bins, LAGS)
    block = lax.slice_in_dim(panel, 0, share_rows * lax.axis_size("narrow"), axis=0)
    spectra_x = cross_spectra(whitened, block, seg_count)
    flat = spectra_x.reshape(share_rows * lax.axis_size("narrow") * ch_count, 2 * slice_bins)
    product = jnp.dot(flat, table_part, preferred_element_type=jnp.float32) * norm_factor
    return lax.psum_scatter(
        product.reshape(share_rows * lax.axis_size("narrow"), ch_count, LAGS),
        "narrow",
        scatter_dimension=0,
        tiled=True,
    )


CHUNKS = 4
STEP = 128


def sincos(residue):
    quadrant = (residue + NSAMP // 8) >> (NSAMP // 4).bit_length() - 1
    x = (residue - quadrant * (NSAMP // 4)).astype(jnp.float32) * (2.0 * math.pi / NSAMP)
    y = x * x
    s = x * (1.0 + y * (-1.0 / 6 + y * (1.0 / 120 + y * (-1.0 / 5040 + y * (1.0 / 362880)))))
    c = 1.0 + y * (-0.5 + y * (1.0 / 24 + y * (-1.0 / 720 + y * (1.0 / 40320))))
    odd = (quadrant & 1) == 1
    sine = jnp.where(odd, c, s)
    cosine = jnp.where(odd, s, c)
    sine = jnp.where((quadrant & 2) == 2, -sine, sine)
    cosine = jnp.where(((quadrant + 1) & 2) == 2, -cosine, cosine)
    return cosine, sine


def kernel(
    x_ref, off_ref, dead_ref, src_ref, o_ref,
    amp, halo, white, chan, panel, table, rows, ca, sa, cb, sb,
    halo_sem, send, recv, white_recv,
):
    half = x_ref.shape[1]
    bins = 2 * half
    part = bins // CHUNKS
    lags = o_ref.shape[1]
    w = lax.axis_index("wide")
    n = lax.axis_index("narrow")
    z = w // 4
    x = (w // 2) % 2
    c = w % 2
    rank = z + n * (3 - 2 * z)
    def device(zv, xv, cv):
        return {"wide": zv * 4 + xv * 2 + cv, "narrow": n}

    def ranked(k):
        return device(k + n * (3 - 2 * k), x, c)

    x_peer, core_peer = device(z, 1 - x, c), device(z, x, 1 - c)
    y_peer = {"wide": w, "narrow": 1 - n}

    def slot(role, xv, cv):
        return (n if role == 0 else 1 - n) * 4 + xv * 2 + cv

    def chunk(q):
        return q + n * (3 - 2 * q)

    barrier = pltpu.get_barrier_semaphore()
    for peer in (y_peer, x_peer, core_peer):
        pl.semaphore_signal(barrier, inc=1, device_id=peer, device_id_type=MESH)

    for k, others in enumerate(((1, 2), (0, 2), (0, 1, 3), (2,))):
        @pl.when(rank == k)
        def _():
            for other in others:
                pl.semaphore_signal(
                    barrier, inc=1, device_id=ranked(other), device_id_type=MESH
                )

    def amplitude(cells):
        re = cells[0:16].astype(jnp.float32)
        im = cells[16:32].astype(jnp.float32)
        size = jnp.sqrt(re * re + im * im)
        high = size.astype(jnp.bfloat16)
        return high, (size - high.astype(jnp.float32)).astype(jnp.bfloat16)

    zeros = jnp.zeros((32, STEP), jnp.bfloat16)
    amp[:, 0:STEP] = zeros
    amp[:, STEP + half : 2 * STEP + half] = zeros
    high, low = amplitude(x_ref[...])
    amp[0:16, STEP : STEP + half] = high
    amp[16:32, STEP : STEP + half] = low

    ahead = lax.broadcasted_iota(jnp.int32, (3 * STEP, STEP), 0) - STEP
    ahead = ahead - lax.broadcasted_iota(jnp.int32, (3 * STEP, STEP), 1)
    band = jnp.where(jnp.abs(ahead) <= SMOOTH, 1.0, 0.0).astype(jnp.bfloat16)

    line = lax.broadcasted_iota(jnp.int32, (16, STEP), 0)
    offsets = jnp.zeros((16, STEP), jnp.int32)
    live = jnp.zeros((16, STEP), jnp.int32)
    for ch in range(6):
        live = jnp.where((line & 7) == ch, dead_ref[ch], live)
        for k in range(2):
            offsets = jnp.where(line == k * 8 + ch, off_ref[k, ch], offsets)
    offsets = offsets[:, 0:1]
    live = live[:, 0:1].astype(jnp.float32)
    line = lax.broadcasted_iota(jnp.int32, (112, 32), 0)
    wanted = (line >> 4) - 1
    for r in range(4):
        wanted = jnp.where((line & 3) + (line >> 4) * 4 == r, src_ref[w * 4 + r] - w * 6, wanted)
    wanted = wanted + ((line & 15) >> 2) * 8
    column = lax.broadcasted_iota(jnp.int32, (112, 32), 1)
    pick = jnp.where(wanted == column, 1.0, 0.0).astype(jnp.bfloat16)

    pl.semaphore_wait(barrier, 5 + (rank // 2) * (5 - 2 * rank))

    edge = pl.ds(pl.multiple_of((1 - n) * (half - STEP), STEP), STEP)
    halo_copy = pltpu.make_async_remote_copy(
        src_ref=x_ref.at[:, edge],
        dst_ref=halo,
        send_sem=halo_sem.at[0],
        recv_sem=halo_sem.at[1],
        device_id=y_peer,
        device_id_type=MESH,
    )
    halo_copy.start()

    def remote(q, at_slot, kind, target):
        return pltpu.make_async_remote_copy(
            src_ref=panel.at[chunk(q), at_slot],
            dst_ref=panel.at[chunk(q), at_slot],
            send_sem=send.at[q, kind],
            recv_sem=recv.at[chunk(q), at_slot],
            device_id=target,
            device_id_type=MESH,
        )

    def white_copy(q, g):
        return pltpu.make_async_remote_copy(
            src_ref=white.at[g],
            dst_ref=white.at[g],
            send_sem=send.at[q, 10],
            recv_sem=white_recv.at[g],
            device_id=y_peer,
            device_id_type=MESH,
        )

    def spread(q, role):
        remote(q, slot(role, x, c), 4 + role, x_peer).start()
        remote(q, slot(role, x, c), 6 + role, core_peer).start()

    def arrived(q, at_slot):
        remote(q, at_slot, 0, core_peer).wait_recv()

    def choose(q, cells):
        picked = jnp.dot(pick, cells, preferred_element_type=jnp.float32)
        mine = picked[0:16].astype(jnp.bfloat16)
        for role in range(2):
            @pl.when(rank == role)
            def _():
                panel[chunk(q), slot(role, x, c)] = mine
                remote(q, slot(role, x, c), 1, ranked(2)).start()
                remote(q, slot(role, x, c), 0, ranked(1 - role)).start()
                spread(q, role)
        chan[chunk(q)] = picked[16:]

    def whiten(q):
        blocks = part // STEP
        g = chunk(q)
        start = (g - 2 * n) * part
        lhs = jnp.concatenate(
            [
                amp[:, pl.ds(pl.multiple_of(start + b * STEP, STEP), 3 * STEP)]
                for b in range(blocks)
            ],
            axis=0,
        )
        sums = jnp.dot(lhs, band, preferred_element_type=jnp.float32)
        windowed = jnp.concatenate(
            [sums[b * 32 : b * 32 + 16] + sums[b * 32 + 16 : b * 32 + 32] for b in range(blocks)],
            axis=1,
        )
        lanes = pl.ds(pl.multiple_of(start, STEP), part)
        re = x_ref[0:16, lanes].astype(jnp.float32)
        im = x_ref[16:32, lanes].astype(jnp.float32)
        f = lax.broadcasted_iota(jnp.int32, (16, part), 1) + g * part
        counts = jnp.minimum(f + SMOOTH, bins - 1) - jnp.maximum(f - SMOOTH, 0) + 1
        smoothed = windowed / counts.astype(jnp.float32) + EPSILON
        cosine, sine = sincos(((f + 1) * offsets) & (NSAMP - 1))
        scale = live / smoothed
        cells = jnp.concatenate(
            [
                ((re * cosine - im * sine) * scale).astype(jnp.bfloat16),
                ((re * sine + im * cosine) * scale).astype(jnp.bfloat16),
            ],
            axis=0,
        )
        white[g] = cells
        white_copy(q, g).start()
        choose(q, cells)

    def along_y(q):
        g = chunk(q)
        white_copy(q, g).wait_recv()
        choose(q, white[g])

    def along_z(q):
        for role in range(2):
            @pl.when(rank == 1 - role)
            def _():
                arrived(q, slot(role, x, c))
                spread(q, role)

        @pl.when(rank == 2)
        def _():
            for role in (1, 0):
                arrived(q, slot(role, x, c))
                remote(q, slot(role, x, c), 2 + role, ranked(3)).start()
                spread(q, role)

        @pl.when(rank == 3)
        def _():
            for role in (1, 0):
                arrived(q, slot(role, x, c))
                spread(q, role)

    def along_x(q):
        for role in range(2):
            arrived(q, slot(role, 1 - x, c))
            remote(q, slot(role, 1 - x, c), 8 + role, core_peer).start()

    def lag_steps(count):
        lag = lax.broadcasted_iota(jnp.int32, (count, lags), 1)
        return lag + (NSAMP - lags // 2), lax.broadcasted_iota(jnp.int32, (count, lags), 0)

    def table_base():
        steps, at = lag_steps(bins // STEP)
        ca[...], sa[...] = sincos((steps * at * STEP) & (NSAMP - 1))
        steps, at = lag_steps(STEP)
        cb[...], sb[...] = sincos((steps * (at + 1)) & (NSAMP - 1))

    def table_part(q):
        first = chunk(q) * (part // STEP)

        def table_step(i, carry):
            a = first + i
            c1 = ca[pl.ds(a, 1), :]
            s1 = sa[pl.ds(a, 1), :]
            for r in range(0, STEP, 16):
                c2 = cb[r : r + 16, :]
                s2 = sb[r : r + 16, :]
                top = pl.ds(pl.multiple_of(a * 2 * STEP + r, 16), 16)
                low = pl.ds(pl.multiple_of(a * 2 * STEP + STEP + r, 16), 16)
                table[top, :] = (c1 * c2 - s1 * s2).astype(jnp.bfloat16)
                table[low, :] = (-s1 * c2 - c1 * s2).astype(jnp.bfloat16)
            return carry

        lax.fori_loop(0, part // STEP, table_step, 0)

    def correlate(q):
        for role in range(2):
            for xv in range(2):
                arrived(q, slot(role, xv, 1 - c))
        g = chunk(q)
        first = lax.broadcasted_iota(jnp.int32, (8, STEP), 0) < 4
        norm = 1.0 / math.sqrt(2)

        def cross(a, carry):
            lanes = pl.ds(pl.multiple_of(a * STEP, STEP), STEP)
            source = [panel[g, b, :, lanes].astype(jnp.float32) for b in range(8)]
            for ch in range(6):
                own = chan[g, ch * 16 : ch * 16 + 16, lanes]
                cr, ci = own[0:8], own[8:16]
                for imag in range(2):
                    terms = []
                    for b in range(8):
                        sr, si = source[b][0:8], source[b][8:16]
                        terms.append(sr * ci - si * cr if imag else sr * cr + si * ci)
                    pairs = []
                    for b in range(0, 8, 2):
                        keep = jnp.where(first, terms[b], terms[b + 1])
                        move = jnp.where(first, terms[b + 1], terms[b])
                        pairs.append(keep + pltpu.roll(move, 4, 0))
                    joined = jnp.concatenate(pairs, axis=0) * norm
                    cols = pl.ds(pl.multiple_of((2 * a + imag) * STEP, STEP), STEP)
                    rows[ch * 32 : ch * 32 + 32, cols] = joined.astype(jnp.bfloat16)
            return carry

        lax.fori_loop(0, part // STEP, cross, 0)
        product = jnp.dot(
            rows[...],
            table[pl.ds(pl.multiple_of(g * 2 * part, 16), 2 * part), :],
            preferred_element_type=jnp.float32,
        ) * (1.0 / math.sqrt(bins))
        if q == 0:
            o_ref[...] = product
        else:
            o_ref[...] += product

    whiten(0)
    table_base()
    halo_copy.wait()
    high, low = amplitude(halo[...])
    edge = pl.ds(pl.multiple_of((1 - n) * (half + STEP), STEP), STEP)
    amp[0:16, edge] = high
    amp[16:32, edge] = low
    whiten(1)
    along_y(3)
    along_y(2)
    along_z(0)
    table_part(0)
    along_z(1)
    along_x(0)
    table_part(1)
    along_z(3)
    along_x(1)
    table_part(3)
    correlate(0)
    along_z(2)
    along_x(3)
    table_part(2)
    correlate(1)
    along_x(2)
    correlate(3)
    correlate(2)

    def sent(q, kind):
        remote(q, 0, kind, core_peer).wait_send()

    for q in range(CHUNKS):
        @pl.when(rank < 2)
        def _():
            sent(q, 0)
            sent(q, 1)

        @pl.when(rank == 2)
        def _():
            sent(q, 2)
            sent(q, 3)

        for kind in range(4, 10):
            sent(q, kind)
    for q in range(2):
        white_copy(q, chunk(q)).wait_send()


def fused_body(spectra, dead_mask, seg_offsets, src_index):
    ch_count, seg_count, _, half = spectra.shape
    bins = 2 * half
    part = bins // CHUNKS
    spare = 8 - ch_count
    cells = jnp.pad(spectra.transpose(2, 1, 0, 3), ((0, 0), (0, 0), (0, spare), (0, 0)))
    cells = cells.reshape(32, half)
    shares = src_index.shape[0] // 2
    vmem = pl.BlockSpec(memory_space=pltpu.VMEM)
    smem = pl.BlockSpec(memory_space=pltpu.SMEM)
    f32, bf16 = jnp.float32, jnp.bfloat16
    result = pl.pallas_call(
        kernel,
        out_shape=jax.ShapeDtypeStruct((ch_count * shares, LAGS), f32),
        in_specs=[vmem, smem, smem, smem],
        out_specs=vmem,
        scratch_shapes=[
            pltpu.VMEM((32, half + 2 * STEP), bf16),
            pltpu.VMEM((32, STEP), bf16),
            pltpu.VMEM((CHUNKS, 32, part), bf16),
            pltpu.VMEM((CHUNKS, ch_count * 16, part), f32),
            pltpu.VMEM((CHUNKS, 8, 16, part), bf16),
            pltpu.VMEM((2 * bins, LAGS), bf16),
            pltpu.VMEM((ch_count * shares, 2 * part), bf16),
            pltpu.VMEM((bins // STEP, LAGS), f32),
            pltpu.VMEM((bins // STEP, LAGS), f32),
            pltpu.VMEM((STEP, LAGS), f32),
            pltpu.VMEM((STEP, LAGS), f32),
            pltpu.SemaphoreType.DMA((2,)),
            pltpu.SemaphoreType.DMA((CHUNKS, 11)),
            pltpu.SemaphoreType.DMA((CHUNKS, 8)),
            pltpu.SemaphoreType.DMA((CHUNKS,)),
        ],
        compiler_params=pltpu.CompilerParams(
            collective_id=0, has_side_effects=True, vmem_limit_bytes=40 * 1024 * 1024
        ),
    )(cells, seg_offsets.T, dead_mask, src_index)
    return result.reshape(ch_count, shares, LAGS).transpose(1, 0, 2)


def solution(mesh):
    placed = (P("wide", None, None, "narrow"), P("wide"), P("wide", None), P())
    fits = mesh.shape["wide"] == 16 and mesh.shape["narrow"] == 2
    return jax.shard_map(
        fused_body if fits else body,
        mesh=mesh,
        in_specs=placed,
        out_specs=P("narrow", "wide", None),
        check_vma=False,
    )
```

```python
import math

import jax
import jax.numpy as jnp
from jax import lax
from jax.experimental import pallas as pl
from jax.experimental.pallas import tpu as pltpu
from jax.sharding import PartitionSpec as P

NSAMP = 32768
LAGS = 512
SMOOTH = 64


EPSILON = 1e-06
MESH = pl.DeviceIdType.MESH


def padded_2(cells, sides, width):
    for axis, dim in sides:
        count = lax.axis_size(axis)
        ends = count - 1
        head = lax.slice_in_dim(cells, 0, width, axis=dim)
        tail = lax.slice_in_dim(cells, cells.shape[dim] - width, cells.shape[dim], axis=dim)
        cells = jnp.concatenate(
            [
                lax.ppermute(tail, axis, [(i, (i + 1) % count) for i in range(ends)]),
                cells,
                lax.ppermute(head, axis, [((i + 1) % count, i) for i in range(ends)]),
            ],
            axis=dim,
        )
    return cells


def window_sums(padded, bins):
    step = 2 * SMOOTH
    blocks = bins // step
    head = padded[..., :bins].reshape(padded.shape[:-1] + (blocks, step))
    tail = padded[..., step:].reshape(padded.shape[:-1] + (blocks, step))
    cells = jnp.concatenate([head, tail], axis=-1)
    ahead = jnp.arange(2 * step)[:, None] - jnp.arange(step)[None, :]
    band = ((ahead >= 0) & (ahead <= step)).astype(jnp.float32)
    sums = jnp.einsum("ckbi,io->ckbo", cells, band, precision=lax.Precision.HIGHEST)
    return sums.reshape(padded.shape[:-1] + (bins,))


def turns(product):
    angles = 2.0 * math.pi / NSAMP * (product % NSAMP).astype(jnp.float32)
    return jnp.cos(angles), jnp.sin(angles)


def lag_table(first, length, lag_count):
    step = 128
    lag_steps = jnp.arange(lag_count, dtype=jnp.int32) - lag_count // 2 + NSAMP
    coarse = first + step * jnp.arange(length // step, dtype=jnp.int32)
    fine = jnp.arange(step, dtype=jnp.int32) + 1
    ca, sa = turns(coarse[:, None] * lag_steps[None, :])
    cb, sb = turns(fine[:, None] * lag_steps[None, :])
    cosine = ca[:, None] * cb[None] - sa[:, None] * sb[None]
    sine = sa[:, None] * cb[None] + ca[:, None] * sb[None]
    return jnp.concatenate(
        [cosine.reshape(length, lag_count), -sine.reshape(length, lag_count)], axis=0
    ).astype(jnp.bfloat16)


def apply_whitening(real_part, imag_part, windowed, freq_bins, total_bins, dead_mask, seg_offsets):
    counts = (
        jnp.minimum(freq_bins + SMOOTH, total_bins - 1) - jnp.maximum(freq_bins - SMOOTH, 0) + 1
    ).astype(jnp.float32)
    smoothed = windowed / counts + EPSILON
    residue = (freq_bins + 1)[None, None, :] * seg_offsets[:, :, None] % NSAMP
    phase = 2.0 * math.pi / NSAMP * residue.astype(jnp.float32)
    scale = dead_mask.astype(jnp.float32)[:, None, None] / smoothed
    cosine = jnp.cos(phase)
    sine = jnp.sin(phase)
    white_real = (real_part * cosine - imag_part * sine) * scale
    white_imag = (real_part * sine + imag_part * cosine) * scale
    return jnp.stack([white_real, white_imag], axis=2).astype(jnp.bfloat16)


def cross_spectra(channels, sources, seg_count):
    chan_real = channels[:, :, 0]
    chan_imag = channels[:, :, 1]
    src_real = sources[:, :, 0]
    src_imag = sources[:, :, 1]
    cross_real = jnp.einsum(
        "ckf,skf->scf", chan_real, src_real, preferred_element_type=jnp.float32
    ) + jnp.einsum("ckf,skf->scf", chan_imag, src_imag, preferred_element_type=jnp.float32)
    cross_imag = jnp.einsum(
        "ckf,skf->scf", chan_imag, src_real, preferred_element_type=jnp.float32
    ) - jnp.einsum("ckf,skf->scf", chan_real, src_imag, preferred_element_type=jnp.float32)
    joined = jnp.concatenate([cross_real, cross_imag], axis=-1) * (1.0 / math.sqrt(seg_count))
    return joined.astype(jnp.bfloat16)


def body(spectra, dead_mask, seg_offsets, src_index):
    ch_count = spectra.shape[0]
    seg_count = spectra.shape[1]
    slice_bins = spectra.shape[3]
    narrow_count = lax.axis_size("narrow")
    wide_count = lax.axis_size("wide")
    total_bins = slice_bins * narrow_count
    narrow_pos = lax.axis_index("narrow")
    wide_pos = lax.axis_index("wide")
    freq_bins = narrow_pos * slice_bins + jnp.arange(slice_bins, dtype=jnp.int32)
    real_part = spectra[:, :, 0].astype(jnp.float32)
    imag_part = spectra[:, :, 1].astype(jnp.float32)
    amplitude = jnp.sqrt(real_part * real_part + imag_part * imag_part)
    padded = padded_2(amplitude, (("narrow", 2),), SMOOTH)
    windowed = window_sums(padded, slice_bins)
    whitened = apply_whitening(
        real_part, imag_part, windowed, freq_bins, total_bins, dead_mask, seg_offsets
    )
    per_block = src_index.shape[0] // wide_count
    own_rows = (
        lax.dynamic_slice_in_dim(src_index, wide_pos * per_block, per_block) - wide_pos * ch_count
    )
    selector = (own_rows[:, None] == jnp.arange(ch_count, dtype=jnp.int32)[None, :]).astype(
        jnp.bfloat16
    )
    chosen = jnp.einsum(
        "rc,ckqf->rkqf", selector, whitened, preferred_element_type=jnp.float32
    ).astype(jnp.bfloat16)
    share_rows = src_index.shape[0] // narrow_count
    norm_factor = 1.0 / math.sqrt(total_bins)
    panel = lax.all_gather(chosen, "wide", axis=0, tiled=True)
    table_part = lag_table(narrow_pos * slice_bins, slice_bins, LAGS)
    block = lax.slice_in_dim(panel, 0, share_rows * lax.axis_size("narrow"), axis=0)
    spectra_x = cross_spectra(whitened, block, seg_count)
    flat = spectra_x.reshape(share_rows * lax.axis_size("narrow") * ch_count, 2 * slice_bins)
    product = jnp.dot(flat, table_part, preferred_element_type=jnp.float32) * norm_factor
    return lax.psum_scatter(
        product.reshape(share_rows * lax.axis_size("narrow"), ch_count, LAGS),
        "narrow",
        scatter_dimension=0,
        tiled=True,
    )


CHUNKS = 4
ORDER = (0, 1, 3, 2)
STEP = 128


def sincos(residue):
    quadrant = (residue + NSAMP // 8) >> (NSAMP // 4).bit_length() - 1
    x = (residue - quadrant * (NSAMP // 4)).astype(jnp.float32) * (2.0 * math.pi / NSAMP)
    y = x * x
    s = x * (1.0 + y * (-1.0 / 6 + y * (1.0 / 120 + y * (-1.0 / 5040 + y * (1.0 / 362880)))))
    c = 1.0 + y * (-0.5 + y * (1.0 / 24 + y * (-1.0 / 720 + y * (1.0 / 40320))))
    odd = (quadrant & 1) == 1
    sine = jnp.where(odd, c, s)
    cosine = jnp.where(odd, s, c)
    sine = jnp.where((quadrant & 2) == 2, -sine, sine)
    cosine = jnp.where(((quadrant + 1) & 2) == 2, -cosine, cosine)
    return cosine, sine


def kernel(
    x_ref, off_ref, dead_ref, src_ref, o_ref,
    amp, halo, white, chan, panel, table, rows, ca, sa, cb, sb,
    halo_sem, send, recv, white_recv,
):
    half = x_ref.shape[1]
    bins = 2 * half
    part = bins // CHUNKS
    lags = o_ref.shape[1]
    w = lax.axis_index("wide")
    n = lax.axis_index("narrow")
    z = w // 4
    x = (w // 2) % 2
    c = w % 2
    rank = z + n * (3 - 2 * z)
    def device(zv, xv, cv):
        return {"wide": zv * 4 + xv * 2 + cv, "narrow": n}

    def ranked(k):
        return device(k + n * (3 - 2 * k), x, c)

    x_peer, core_peer = device(z, 1 - x, c), device(z, x, 1 - c)
    y_peer = {"wide": w, "narrow": 1 - n}

    def slot(role, xv, cv):
        return (n if role == 0 else 1 - n) * 4 + xv * 2 + cv

    def chunk(q):
        return q + n * (3 - 2 * q)

    barrier = pltpu.get_barrier_semaphore()
    for peer in (y_peer, x_peer, core_peer):
        pl.semaphore_signal(barrier, inc=1, device_id=peer, device_id_type=MESH)

    for k, others in enumerate(((1, 2), (0, 2), (0, 1, 3), (2,))):
        @pl.when(rank == k)
        def _():
            for other in others:
                pl.semaphore_signal(
                    barrier, inc=1, device_id=ranked(other), device_id_type=MESH
                )

    def amplitude(cells):
        re = cells[0:16].astype(jnp.float32)
        im = cells[16:32].astype(jnp.float32)
        size = jnp.sqrt(re * re + im * im)
        high = size.astype(jnp.bfloat16)
        return high, (size - high.astype(jnp.float32)).astype(jnp.bfloat16)

    zeros = jnp.zeros((32, STEP), jnp.bfloat16)
    amp[:, 0:STEP] = zeros
    amp[:, STEP + half : 2 * STEP + half] = zeros
    high, low = amplitude(x_ref[...])
    amp[0:16, STEP : STEP + half] = high
    amp[16:32, STEP : STEP + half] = low

    ahead = lax.broadcasted_iota(jnp.int32, (3 * STEP, STEP), 0) - STEP
    ahead = ahead - lax.broadcasted_iota(jnp.int32, (3 * STEP, STEP), 1)
    band = jnp.where(jnp.abs(ahead) <= SMOOTH, 1.0, 0.0).astype(jnp.bfloat16)

    line = lax.broadcasted_iota(jnp.int32, (16, STEP), 0)
    offsets = jnp.zeros((16, STEP), jnp.int32)
    live = jnp.zeros((16, STEP), jnp.int32)
    for ch in range(6):
        live = jnp.where((line & 7) == ch, dead_ref[ch], live)
        for k in range(2):
            offsets = jnp.where(line == k * 8 + ch, off_ref[k, ch], offsets)
    offsets = offsets[:, 0:1]
    live = live[:, 0:1].astype(jnp.float32)
    line = lax.broadcasted_iota(jnp.int32, (112, 32), 0)
    wanted = (line >> 4) - 1
    for r in range(4):
        wanted = jnp.where((line & 3) + (line >> 4) * 4 == r, src_ref[w * 4 + r] - w * 6, wanted)
    wanted = wanted + ((line & 15) >> 2) * 8
    column = lax.broadcasted_iota(jnp.int32, (112, 32), 1)
    pick = jnp.where(wanted == column, 1.0, 0.0).astype(jnp.bfloat16)

    pl.semaphore_wait(barrier, 5 + (rank // 2) * (5 - 2 * rank))

    edge = pl.ds(pl.multiple_of((1 - n) * (half - STEP), STEP), STEP)
    halo_copy = pltpu.make_async_remote_copy(
        src_ref=x_ref.at[:, edge],
        dst_ref=halo,
        send_sem=halo_sem.at[0],
        recv_sem=halo_sem.at[1],
        device_id=y_peer,
        device_id_type=MESH,
    )
    halo_copy.start()

    def remote(q, at_slot, kind, target):
        return pltpu.make_async_remote_copy(
            src_ref=panel.at[chunk(q), at_slot],
            dst_ref=panel.at[chunk(q), at_slot],
            send_sem=send.at[q, kind],
            recv_sem=recv.at[chunk(q), at_slot],
            device_id=target,
            device_id_type=MESH,
        )

    def white_copy(q, g):
        return pltpu.make_async_remote_copy(
            src_ref=white.at[g],
            dst_ref=white.at[g],
            send_sem=send.at[q, 10],
            recv_sem=white_recv.at[g],
            device_id=y_peer,
            device_id_type=MESH,
        )

    def spread(q, role):
        remote(q, slot(role, x, c), 4 + role, x_peer).start()
        remote(q, slot(role, x, c), 6 + role, core_peer).start()

    def arrived(q, at_slot):
        remote(q, at_slot, 0, core_peer).wait_recv()

    def choose(q, cells):
        picked = jnp.dot(pick, cells, preferred_element_type=jnp.float32)
        mine = picked[0:16].astype(jnp.bfloat16)
        for role in range(2):
            @pl.when(rank == role)
            def _():
                panel[chunk(q), slot(role, x, c)] = mine
                remote(q, slot(role, x, c), 1, ranked(2)).start()
                remote(q, slot(role, x, c), 0, ranked(1 - role)).start()
                spread(q, role)
        chan[chunk(q)] = picked[16:] * (1.0 / math.sqrt(2))

    def whiten(q):
        blocks = part // STEP
        g = chunk(q)
        start = (g - 2 * n) * part
        lhs = jnp.concatenate(
            [
                amp[:, pl.ds(pl.multiple_of(start + b * STEP, STEP), 3 * STEP)]
                for b in range(blocks)
            ],
            axis=0,
        )
        sums = jnp.dot(lhs, band, preferred_element_type=jnp.float32)
        windowed = jnp.concatenate(
            [sums[b * 32 : b * 32 + 16] + sums[b * 32 + 16 : b * 32 + 32] for b in range(blocks)],
            axis=1,
        )
        lanes = pl.ds(pl.multiple_of(start, STEP), part)
        re = x_ref[0:16, lanes].astype(jnp.float32)
        im = x_ref[16:32, lanes].astype(jnp.float32)
        f = lax.broadcasted_iota(jnp.int32, (16, part), 1) + g * part
        counts = jnp.minimum(f + SMOOTH, bins - 1) - jnp.maximum(f - SMOOTH, 0) + 1
        smoothed = windowed / counts.astype(jnp.float32) + EPSILON
        cosine, sine = sincos(((f + 1) * offsets) & (NSAMP - 1))
        scale = live / smoothed
        cells = jnp.concatenate(
            [
                ((re * cosine - im * sine) * scale).astype(jnp.bfloat16),
                ((re * sine + im * cosine) * scale).astype(jnp.bfloat16),
            ],
            axis=0,
        )
        white[g] = cells
        white_copy(q, g).start()
        choose(q, cells)

    def along_y(q):
        g = chunk(q)
        white_copy(q, g).wait_recv()
        choose(q, white[g])

    def along_z(q):
        for role in range(2):
            @pl.when(rank == 1 - role)
            def _():
                arrived(q, slot(role, x, c))
                spread(q, role)

        @pl.when(rank == 2)
        def _():
            for role in (1, 0):
                arrived(q, slot(role, x, c))
                remote(q, slot(role, x, c), 2 + role, ranked(3)).start()
                spread(q, role)

        @pl.when(rank == 3)
        def _():
            for role in (1, 0):
                arrived(q, slot(role, x, c))
                spread(q, role)

    def along_x(q):
        for role in range(2):
            arrived(q, slot(role, 1 - x, c))
            remote(q, slot(role, 1 - x, c), 8 + role, core_peer).start()

    def lag_steps(count):
        lag = lax.broadcasted_iota(jnp.int32, (count, lags), 1)
        return lag + (NSAMP - lags // 2), lax.broadcasted_iota(jnp.int32, (count, lags), 0)

    def table_base():
        steps, at = lag_steps(bins // STEP)
        ca[...], sa[...] = sincos((steps * at * STEP) & (NSAMP - 1))
        steps, at = lag_steps(STEP)
        cb[...], sb[...] = sincos((steps * (at + 1)) & (NSAMP - 1))

    def table_part(q):
        first = chunk(q) * (part // STEP)

        def table_step(i, carry):
            a = first + i
            c1 = ca[pl.ds(a, 1), :]
            s1 = sa[pl.ds(a, 1), :]
            for r in range(0, STEP, 16):
                c2 = cb[r : r + 16, :]
                s2 = sb[r : r + 16, :]
                top = pl.ds(pl.multiple_of(a * 2 * STEP + r, 16), 16)
                low = pl.ds(pl.multiple_of(a * 2 * STEP + STEP + r, 16), 16)
                table[top, :] = (c1 * c2 - s1 * s2).astype(jnp.bfloat16)
                table[low, :] = (-s1 * c2 - c1 * s2).astype(jnp.bfloat16)
            return carry

        lax.fori_loop(0, part // STEP, table_step, 0)

    def multiply(place):
        g = chunk(ORDER[place])
        product = jnp.dot(
            rows[place % 2],
            table[pl.ds(pl.multiple_of(g * 2 * part, 16), 2 * part), :],
            preferred_element_type=jnp.float32,
        ) * (1.0 / math.sqrt(bins))
        if place == 0:
            o_ref[...] = product
        else:
            o_ref[...] += product

    def correlate(place):
        q = ORDER[place]
        for role in range(2):
            for xv in range(2):
                arrived(q, slot(role, xv, 1 - c))
        g = chunk(q)
        first = lax.broadcasted_iota(jnp.int32, (8, STEP), 0) < 4

        def cross(a, carry):
            lanes = pl.ds(pl.multiple_of(a * STEP, STEP), STEP)
            source = [panel[g, b, :, lanes].astype(jnp.float32) for b in range(8)]
            for ch in range(6):
                own = chan[g, ch * 16 : ch * 16 + 16, lanes]
                cr, ci = own[0:8], own[8:16]
                for imag in range(2):
                    terms = []
                    for b in range(8):
                        sr, si = source[b][0:8], source[b][8:16]
                        terms.append(sr * ci - si * cr if imag else sr * cr + si * ci)
                    pairs = []
                    for b in range(0, 8, 2):
                        keep = jnp.where(first, terms[b], terms[b + 1])
                        move = jnp.where(first, terms[b + 1], terms[b])
                        pairs.append(keep + pltpu.roll(move, 4, 0))
                    joined = jnp.concatenate(pairs, axis=0)
                    cols = pl.ds(pl.multiple_of((2 * a + imag) * STEP, STEP), STEP)
                    rows[place % 2, ch * 32 : ch * 32 + 32, cols] = joined.astype(jnp.bfloat16)
            return carry

        if place > 0:
            multiply(place - 1)
        lax.fori_loop(0, part // STEP, cross, 0, unroll=True)

    whiten(0)
    table_base()
    table_part(0)
    halo_copy.wait()
    high, low = amplitude(halo[...])
    edge = pl.ds(pl.multiple_of((1 - n) * (half + STEP), STEP), STEP)
    amp[0:16, edge] = high
    amp[16:32, edge] = low
    whiten(1)
    table_part(1)
    along_y(3)
    along_y(2)
    along_z(0)
    along_z(1)
    along_x(0)
    table_part(3)
    along_z(3)
    along_x(1)
    along_z(2)
    along_x(3)
    correlate(0)
    table_part(2)
    along_x(2)
    correlate(1)
    correlate(2)
    correlate(3)
    multiply(3)

    def sent(q, kind):
        remote(q, 0, kind, core_peer).wait_send()

    for q in range(CHUNKS):
        @pl.when(rank < 2)
        def _():
            sent(q, 0)
            sent(q, 1)

        @pl.when(rank == 2)
        def _():
            sent(q, 2)
            sent(q, 3)

        for kind in range(4, 10):
            sent(q, kind)
    for q in range(2):
        white_copy(q, chunk(q)).wait_send()


def fused_body(spectra, dead_mask, seg_offsets, src_index):
    ch_count, seg_count, _, half = spectra.shape
    bins = 2 * half
    part = bins // CHUNKS
    spare = 8 - ch_count
    cells = jnp.pad(spectra.transpose(2, 1, 0, 3), ((0, 0), (0, 0), (0, spare), (0, 0)))
    cells = cells.reshape(32, half)
    shares = src_index.shape[0] // 2
    vmem = pl.BlockSpec(memory_space=pltpu.VMEM)
    smem = pl.BlockSpec(memory_space=pltpu.SMEM)
    f32, bf16 = jnp.float32, jnp.bfloat16
    result = pl.pallas_call(
        kernel,
        out_shape=jax.ShapeDtypeStruct((ch_count * shares, LAGS), f32),
        in_specs=[vmem, smem, smem, smem],
        out_specs=vmem,
        scratch_shapes=[
            pltpu.VMEM((32, half + 2 * STEP), bf16),
            pltpu.VMEM((32, STEP), bf16),
            pltpu.VMEM((CHUNKS, 32, part), bf16),
            pltpu.VMEM((CHUNKS, ch_count * 16, part), f32),
            pltpu.VMEM((CHUNKS, 8, 16, part), bf16),
            pltpu.VMEM((2 * bins, LAGS), bf16),
            pltpu.VMEM((2, ch_count * shares, 2 * part), bf16),
            pltpu.VMEM((bins // STEP, LAGS), f32),
            pltpu.VMEM((bins // STEP, LAGS), f32),
            pltpu.VMEM((STEP, LAGS), f32),
            pltpu.VMEM((STEP, LAGS), f32),
            pltpu.SemaphoreType.DMA((2,)),
            pltpu.SemaphoreType.DMA((CHUNKS, 11)),
            pltpu.SemaphoreType.DMA((CHUNKS, 8)),
            pltpu.SemaphoreType.DMA((CHUNKS,)),
        ],
        compiler_params=pltpu.CompilerParams(
            collective_id=0, has_side_effects=True, vmem_limit_bytes=40 * 1024 * 1024
        ),
    )(cells, seg_offsets.T, dead_mask, src_index)
    return result.reshape(ch_count, shares, LAGS).transpose(1, 0, 2)


def solution(mesh):
    placed = (P("wide", None, None, "narrow"), P("wide"), P("wide", None), P())
    fits = mesh.shape["wide"] == 16 and mesh.shape["narrow"] == 2
    return jax.shard_map(
        fused_body if fits else body,
        mesh=mesh,
        in_specs=placed,
        out_specs=P("narrow", "wide", None),
        check_vma=False,
    )
```

```python
import math

import jax
import jax.numpy as jnp
from jax import lax
from jax.experimental import pallas as pl
from jax.experimental.pallas import tpu as pltpu
from jax.sharding import PartitionSpec as P

NSAMP = 32768
LAGS = 512
SMOOTH = 64


EPSILON = 1e-06
MESH = pl.DeviceIdType.MESH


def padded_2(cells, sides, width):
    for axis, dim in sides:
        count = lax.axis_size(axis)
        ends = count - 1
        head = lax.slice_in_dim(cells, 0, width, axis=dim)
        tail = lax.slice_in_dim(cells, cells.shape[dim] - width, cells.shape[dim], axis=dim)
        cells = jnp.concatenate(
            [
                lax.ppermute(tail, axis, [(i, (i + 1) % count) for i in range(ends)]),
                cells,
                lax.ppermute(head, axis, [((i + 1) % count, i) for i in range(ends)]),
            ],
            axis=dim,
        )
    return cells


def window_sums(padded, bins):
    step = 2 * SMOOTH
    blocks = bins // step
    head = padded[..., :bins].reshape(padded.shape[:-1] + (blocks, step))
    tail = padded[..., step:].reshape(padded.shape[:-1] + (blocks, step))
    cells = jnp.concatenate([head, tail], axis=-1)
    ahead = jnp.arange(2 * step)[:, None] - jnp.arange(step)[None, :]
    band = ((ahead >= 0) & (ahead <= step)).astype(jnp.float32)
    sums = jnp.einsum("ckbi,io->ckbo", cells, band, precision=lax.Precision.HIGHEST)
    return sums.reshape(padded.shape[:-1] + (bins,))


def turns(product):
    angles = 2.0 * math.pi / NSAMP * (product % NSAMP).astype(jnp.float32)
    return jnp.cos(angles), jnp.sin(angles)


def lag_table(first, length, lag_count):
    step = 128
    lag_steps = jnp.arange(lag_count, dtype=jnp.int32) - lag_count // 2 + NSAMP
    coarse = first + step * jnp.arange(length // step, dtype=jnp.int32)
    fine = jnp.arange(step, dtype=jnp.int32) + 1
    ca, sa = turns(coarse[:, None] * lag_steps[None, :])
    cb, sb = turns(fine[:, None] * lag_steps[None, :])
    cosine = ca[:, None] * cb[None] - sa[:, None] * sb[None]
    sine = sa[:, None] * cb[None] + ca[:, None] * sb[None]
    return jnp.concatenate(
        [cosine.reshape(length, lag_count), -sine.reshape(length, lag_count)], axis=0
    ).astype(jnp.bfloat16)


def apply_whitening(real_part, imag_part, windowed, freq_bins, total_bins, dead_mask, seg_offsets):
    counts = (
        jnp.minimum(freq_bins + SMOOTH, total_bins - 1) - jnp.maximum(freq_bins - SMOOTH, 0) + 1
    ).astype(jnp.float32)
    smoothed = windowed / counts + EPSILON
    residue = (freq_bins + 1)[None, None, :] * seg_offsets[:, :, None] % NSAMP
    phase = 2.0 * math.pi / NSAMP * residue.astype(jnp.float32)
    scale = dead_mask.astype(jnp.float32)[:, None, None] / smoothed
    cosine = jnp.cos(phase)
    sine = jnp.sin(phase)
    white_real = (real_part * cosine - imag_part * sine) * scale
    white_imag = (real_part * sine + imag_part * cosine) * scale
    return jnp.stack([white_real, white_imag], axis=2).astype(jnp.bfloat16)


def cross_spectra(channels, sources, seg_count):
    chan_real = channels[:, :, 0]
    chan_imag = channels[:, :, 1]
    src_real = sources[:, :, 0]
    src_imag = sources[:, :, 1]
    cross_real = jnp.einsum(
        "ckf,skf->scf", chan_real, src_real, preferred_element_type=jnp.float32
    ) + jnp.einsum("ckf,skf->scf", chan_imag, src_imag, preferred_element_type=jnp.float32)
    cross_imag = jnp.einsum(
        "ckf,skf->scf", chan_imag, src_real, preferred_element_type=jnp.float32
    ) - jnp.einsum("ckf,skf->scf", chan_real, src_imag, preferred_element_type=jnp.float32)
    joined = jnp.concatenate([cross_real, cross_imag], axis=-1) * (1.0 / math.sqrt(seg_count))
    return joined.astype(jnp.bfloat16)


def body(spectra, dead_mask, seg_offsets, src_index):
    ch_count = spectra.shape[0]
    seg_count = spectra.shape[1]
    slice_bins = spectra.shape[3]
    narrow_count = lax.axis_size("narrow")
    wide_count = lax.axis_size("wide")
    total_bins = slice_bins * narrow_count
    narrow_pos = lax.axis_index("narrow")
    wide_pos = lax.axis_index("wide")
    freq_bins = narrow_pos * slice_bins + jnp.arange(slice_bins, dtype=jnp.int32)
    real_part = spectra[:, :, 0].astype(jnp.float32)
    imag_part = spectra[:, :, 1].astype(jnp.float32)
    amplitude = jnp.sqrt(real_part * real_part + imag_part * imag_part)
    padded = padded_2(amplitude, (("narrow", 2),), SMOOTH)
    windowed = window_sums(padded, slice_bins)
    whitened = apply_whitening(
        real_part, imag_part, windowed, freq_bins, total_bins, dead_mask, seg_offsets
    )
    per_block = src_index.shape[0] // wide_count
    own_rows = (
        lax.dynamic_slice_in_dim(src_index, wide_pos * per_block, per_block) - wide_pos * ch_count
    )
    selector = (own_rows[:, None] == jnp.arange(ch_count, dtype=jnp.int32)[None, :]).astype(
        jnp.bfloat16
    )
    chosen = jnp.einsum(
        "rc,ckqf->rkqf", selector, whitened, preferred_element_type=jnp.float32
    ).astype(jnp.bfloat16)
    share_rows = src_index.shape[0] // narrow_count
    norm_factor = 1.0 / math.sqrt(total_bins)
    panel = lax.all_gather(chosen, "wide", axis=0, tiled=True)
    table_part = lag_table(narrow_pos * slice_bins, slice_bins, LAGS)
    block = lax.slice_in_dim(panel, 0, share_rows * lax.axis_size("narrow"), axis=0)
    spectra_x = cross_spectra(whitened, block, seg_count)
    flat = spectra_x.reshape(share_rows * lax.axis_size("narrow") * ch_count, 2 * slice_bins)
    product = jnp.dot(flat, table_part, preferred_element_type=jnp.float32) * norm_factor
    return lax.psum_scatter(
        product.reshape(share_rows * lax.axis_size("narrow"), ch_count, LAGS),
        "narrow",
        scatter_dimension=0,
        tiled=True,
    )


CHUNKS = 4
ORDER = (0, 1, 3, 2)
STEP = 128


def sincos(residue):
    quadrant = (residue + NSAMP // 8) >> (NSAMP // 4).bit_length() - 1
    x = (residue - quadrant * (NSAMP // 4)).astype(jnp.float32) * (2.0 * math.pi / NSAMP)
    y = x * x
    s = x * (1.0 + y * (-1.0 / 6 + y * (1.0 / 120 + y * (-1.0 / 5040 + y * (1.0 / 362880)))))
    c = 1.0 + y * (-0.5 + y * (1.0 / 24 + y * (-1.0 / 720 + y * (1.0 / 40320))))
    odd = (quadrant & 1) == 1
    sine = jnp.where(odd, c, s)
    cosine = jnp.where(odd, s, c)
    sine = jnp.where((quadrant & 2) == 2, -sine, sine)
    cosine = jnp.where(((quadrant + 1) & 2) == 2, -cosine, cosine)
    return cosine, sine


def kernel(
    x_ref, off_ref, dead_ref, src_ref, o_ref,
    amp, halo, white, chan, panel, table, rows, ca, sa, cb, sb,
    halo_sem, send, recv, white_recv,
):
    half = x_ref.shape[1]
    bins = 2 * half
    part = bins // CHUNKS
    lags = o_ref.shape[1]
    w = lax.axis_index("wide")
    n = lax.axis_index("narrow")
    z = w // 4
    x = (w // 2) % 2
    c = w % 2
    rank = z + n * (3 - 2 * z)
    def device(zv, xv, cv):
        return {"wide": zv * 4 + xv * 2 + cv, "narrow": n}

    def ranked(k):
        return device(k + n * (3 - 2 * k), x, c)

    x_peer, core_peer = device(z, 1 - x, c), device(z, x, 1 - c)
    y_peer = {"wide": w, "narrow": 1 - n}

    def slot(role, xv, cv):
        return (n if role == 0 else 1 - n) * 4 + xv * 2 + cv

    def chunk(q):
        return q + n * (3 - 2 * q)

    barrier = pltpu.get_barrier_semaphore()
    for peer in (y_peer, x_peer, core_peer):
        pl.semaphore_signal(barrier, inc=1, device_id=peer, device_id_type=MESH)

    for k, others in enumerate(((1, 2), (0, 2), (0, 1, 3), (2,))):
        @pl.when(rank == k)
        def _():
            for other in others:
                pl.semaphore_signal(
                    barrier, inc=1, device_id=ranked(other), device_id_type=MESH
                )

    def amplitude(cells):
        re = cells[0:16].astype(jnp.float32)
        im = cells[16:32].astype(jnp.float32)
        size = jnp.sqrt(re * re + im * im)
        high = size.astype(jnp.bfloat16)
        return high, (size - high.astype(jnp.float32)).astype(jnp.bfloat16)

    zeros = jnp.zeros((32, STEP), jnp.bfloat16)
    amp[:, 0:STEP] = zeros
    amp[:, STEP + half : 2 * STEP + half] = zeros
    high, low = amplitude(x_ref[...])
    amp[0:16, STEP : STEP + half] = high
    amp[16:32, STEP : STEP + half] = low

    ahead = lax.broadcasted_iota(jnp.int32, (3 * STEP, STEP), 0) - STEP
    ahead = ahead - lax.broadcasted_iota(jnp.int32, (3 * STEP, STEP), 1)
    band = jnp.where(jnp.abs(ahead) <= SMOOTH, 1.0, 0.0).astype(jnp.bfloat16)

    line = lax.broadcasted_iota(jnp.int32, (16, STEP), 0)
    offsets = jnp.zeros((16, STEP), jnp.int32)
    live = jnp.zeros((16, STEP), jnp.int32)
    for ch in range(6):
        live = jnp.where((line & 7) == ch, dead_ref[ch], live)
        for k in range(2):
            offsets = jnp.where(line == k * 8 + ch, off_ref[k, ch], offsets)
    offsets = offsets[:, 0:1]
    live = live[:, 0:1].astype(jnp.float32)
    line = lax.broadcasted_iota(jnp.int32, (112, 32), 0)
    wanted = (line >> 4) - 1
    for r in range(4):
        wanted = jnp.where((line & 3) + (line >> 4) * 4 == r, src_ref[w * 4 + r] - w * 6, wanted)
    wanted = wanted + ((line & 15) >> 2) * 8
    column = lax.broadcasted_iota(jnp.int32, (112, 32), 1)
    pick = jnp.where(wanted == column, 1.0, 0.0).astype(jnp.bfloat16)

    pl.semaphore_wait(barrier, 5 + (rank // 2) * (5 - 2 * rank))

    edge = pl.ds(pl.multiple_of((1 - n) * (half - STEP), STEP), STEP)
    halo_copy = pltpu.make_async_remote_copy(
        src_ref=x_ref.at[:, edge],
        dst_ref=halo,
        send_sem=halo_sem.at[0],
        recv_sem=halo_sem.at[1],
        device_id=y_peer,
        device_id_type=MESH,
    )
    halo_copy.start()

    def remote(q, at_slot, kind, target):
        return pltpu.make_async_remote_copy(
            src_ref=panel.at[chunk(q), at_slot],
            dst_ref=panel.at[chunk(q), at_slot],
            send_sem=send.at[q, kind],
            recv_sem=recv.at[chunk(q), at_slot],
            device_id=target,
            device_id_type=MESH,
        )

    def white_copy(q, g):
        return pltpu.make_async_remote_copy(
            src_ref=white.at[g],
            dst_ref=white.at[g],
            send_sem=send.at[q, 10],
            recv_sem=white_recv.at[g],
            device_id=y_peer,
            device_id_type=MESH,
        )

    def spread(q, role):
        remote(q, slot(role, x, c), 4 + role, x_peer).start()
        remote(q, slot(role, x, c), 6 + role, core_peer).start()

    def arrived(q, at_slot):
        remote(q, at_slot, 0, core_peer).wait_recv()

    def choose(q, cells):
        picked = jnp.dot(pick, cells, preferred_element_type=jnp.float32)
        mine = picked[0:16].astype(jnp.bfloat16)
        for role in range(2):
            @pl.when(rank == role)
            def _():
                panel[chunk(q), slot(role, x, c)] = mine
                remote(q, slot(role, x, c), 1, ranked(2)).start()
                remote(q, slot(role, x, c), 0, ranked(1 - role)).start()
                spread(q, role)
        chan[chunk(q)] = picked[16:] * (1.0 / math.sqrt(2))

    def whiten(q):
        blocks = part // STEP
        g = chunk(q)
        start = (g - 2 * n) * part
        lhs = jnp.concatenate(
            [
                amp[:, pl.ds(pl.multiple_of(start + b * STEP, STEP), 3 * STEP)]
                for b in range(blocks)
            ],
            axis=0,
        )
        sums = jnp.dot(lhs, band, preferred_element_type=jnp.float32)
        windowed = jnp.concatenate(
            [sums[b * 32 : b * 32 + 16] + sums[b * 32 + 16 : b * 32 + 32] for b in range(blocks)],
            axis=1,
        )
        lanes = pl.ds(pl.multiple_of(start, STEP), part)
        re = x_ref[0:16, lanes].astype(jnp.float32)
        im = x_ref[16:32, lanes].astype(jnp.float32)
        f = lax.broadcasted_iota(jnp.int32, (16, part), 1) + g * part
        counts = jnp.minimum(f + SMOOTH, bins - 1) - jnp.maximum(f - SMOOTH, 0) + 1
        smoothed = windowed / counts.astype(jnp.float32) + EPSILON
        cosine, sine = sincos(((f + 1) * offsets) & (NSAMP - 1))
        scale = live / smoothed
        cells = jnp.concatenate(
            [
                ((re * cosine - im * sine) * scale).astype(jnp.bfloat16),
                ((re * sine + im * cosine) * scale).astype(jnp.bfloat16),
            ],
            axis=0,
        )
        white[g] = cells
        white_copy(q, g).start()
        choose(q, cells)

    def along_y(q):
        g = chunk(q)
        white_copy(q, g).wait_recv()
        choose(q, white[g])

    def along_z(q):
        for role in range(2):
            @pl.when(rank == 1 - role)
            def _():
                arrived(q, slot(role, x, c))
                spread(q, role)

        @pl.when(rank == 2)
        def _():
            for role in (1, 0):
                arrived(q, slot(role, x, c))
                remote(q, slot(role, x, c), 2 + role, ranked(3)).start()
                spread(q, role)

        @pl.when(rank == 3)
        def _():
            for role in (1, 0):
                arrived(q, slot(role, x, c))
                spread(q, role)

    def along_x(q):
        for role in range(2):
            arrived(q, slot(role, 1 - x, c))
            remote(q, slot(role, 1 - x, c), 8 + role, core_peer).start()

    def lag_steps(count):
        lag = lax.broadcasted_iota(jnp.int32, (count, lags), 1)
        return lag + (NSAMP - lags // 2), lax.broadcasted_iota(jnp.int32, (count, lags), 0)

    def table_base():
        steps, at = lag_steps(bins // STEP)
        ca[...], sa[...] = sincos((steps * at * STEP) & (NSAMP - 1))
        steps, at = lag_steps(STEP)
        cb[...], sb[...] = sincos((steps * (at + 1)) & (NSAMP - 1))

    def table_part(q):
        first = chunk(q) * (part // STEP)

        def table_step(i, carry):
            a = first + i
            c1 = ca[pl.ds(a, 1), :]
            s1 = sa[pl.ds(a, 1), :]
            for r in range(0, STEP, 16):
                c2 = cb[r : r + 16, :]
                s2 = sb[r : r + 16, :]
                top = pl.ds(pl.multiple_of(a * 2 * STEP + r, 16), 16)
                low = pl.ds(pl.multiple_of(a * 2 * STEP + STEP + r, 16), 16)
                table[top, :] = (c1 * c2 - s1 * s2).astype(jnp.bfloat16)
                table[low, :] = (-s1 * c2 - c1 * s2).astype(jnp.bfloat16)
            return carry

        lax.fori_loop(0, part // STEP, table_step, 0)

    def multiply(place):
        g = chunk(ORDER[place])
        product = jnp.dot(
            rows[place % 2],
            table[pl.ds(pl.multiple_of(g * 2 * part, 16), 2 * part), :],
            preferred_element_type=jnp.float32,
        ) * (1.0 / math.sqrt(bins))
        if place == 0:
            o_ref[...] = product
        else:
            o_ref[...] += product

    def correlate(place):
        q = ORDER[place]
        for role in range(2):
            for xv in range(2):
                arrived(q, slot(role, xv, 1 - c))
        g = chunk(q)
        first = lax.broadcasted_iota(jnp.int32, (8, STEP), 0) < 4

        def cross(a, carry):
            lanes = pl.ds(pl.multiple_of(a * STEP, STEP), STEP)
            source = [panel[g, b, :, lanes].astype(jnp.float32) for b in range(8)]
            for ch in range(6):
                own = chan[g, ch * 16 : ch * 16 + 16, lanes]
                cr, ci = own[0:8], own[8:16]
                for imag in range(2):
                    terms = []
                    for b in range(8):
                        sr, si = source[b][0:8], source[b][8:16]
                        terms.append(sr * ci - si * cr if imag else sr * cr + si * ci)
                    pairs = []
                    for b in range(0, 8, 2):
                        keep = jnp.where(first, terms[b], terms[b + 1])
                        move = jnp.where(first, terms[b + 1], terms[b])
                        pairs.append(keep + pltpu.roll(move, 4, 0))
                    joined = jnp.concatenate(pairs, axis=0)
                    cols = pl.ds(pl.multiple_of((2 * a + imag) * STEP, STEP), STEP)
                    rows[place % 2, ch * 32 : ch * 32 + 32, cols] = joined.astype(jnp.bfloat16)
            return carry

        if place > 0:
            multiply(place - 1)
        lax.fori_loop(0, part // STEP, cross, 0, unroll=True)

    whiten(0)
    table_base()
    table_part(0)
    halo_copy.wait()
    high, low = amplitude(halo[...])
    edge = pl.ds(pl.multiple_of((1 - n) * (half + STEP), STEP), STEP)
    amp[0:16, edge] = high
    amp[16:32, edge] = low
    whiten(1)
    table_part(1)
    along_y(3)
    along_y(2)
    along_z(0)
    along_z(1)
    along_z(3)
    along_z(2)
    along_x(0)
    table_part(3)
    along_x(1)
    along_x(3)
    correlate(0)
    table_part(2)
    along_x(2)
    correlate(1)
    correlate(2)
    correlate(3)
    multiply(3)

    def sent(q, kind):
        remote(q, 0, kind, core_peer).wait_send()

    for q in range(CHUNKS):
        @pl.when(rank < 2)
        def _():
            sent(q, 0)
            sent(q, 1)

        @pl.when(rank == 2)
        def _():
            sent(q, 2)
            sent(q, 3)

        for kind in range(4, 10):
            sent(q, kind)
    for q in range(2):
        white_copy(q, chunk(q)).wait_send()


def fused_body(spectra, dead_mask, seg_offsets, src_index):
    ch_count, seg_count, _, half = spectra.shape
    bins = 2 * half
    part = bins // CHUNKS
    spare = 8 - ch_count
    cells = jnp.pad(spectra.transpose(2, 1, 0, 3), ((0, 0), (0, 0), (0, spare), (0, 0)))
    cells = cells.reshape(32, half)
    shares = src_index.shape[0] // 2
    vmem = pl.BlockSpec(memory_space=pltpu.VMEM)
    smem = pl.BlockSpec(memory_space=pltpu.SMEM)
    f32, bf16 = jnp.float32, jnp.bfloat16
    result = pl.pallas_call(
        kernel,
        out_shape=jax.ShapeDtypeStruct((ch_count * shares, LAGS), f32),
        in_specs=[vmem, smem, smem, smem],
        out_specs=vmem,
        scratch_shapes=[
            pltpu.VMEM((32, half + 2 * STEP), bf16),
            pltpu.VMEM((32, STEP), bf16),
            pltpu.VMEM((CHUNKS, 32, part), bf16),
            pltpu.VMEM((CHUNKS, ch_count * 16, part), f32),
            pltpu.VMEM((CHUNKS, 8, 16, part), bf16),
            pltpu.VMEM((2 * bins, LAGS), bf16),
            pltpu.VMEM((2, ch_count * shares, 2 * part), bf16),
            pltpu.VMEM((bins // STEP, LAGS), f32),
            pltpu.VMEM((bins // STEP, LAGS), f32),
            pltpu.VMEM((STEP, LAGS), f32),
            pltpu.VMEM((STEP, LAGS), f32),
            pltpu.SemaphoreType.DMA((2,)),
            pltpu.SemaphoreType.DMA((CHUNKS, 11)),
            pltpu.SemaphoreType.DMA((CHUNKS, 8)),
            pltpu.SemaphoreType.DMA((CHUNKS,)),
        ],
        compiler_params=pltpu.CompilerParams(
            collective_id=0, has_side_effects=True, vmem_limit_bytes=40 * 1024 * 1024
        ),
    )(cells, seg_offsets.T, dead_mask, src_index)
    return result.reshape(ch_count, shares, LAGS).transpose(1, 0, 2)


def solution(mesh):
    placed = (P("wide", None, None, "narrow"), P("wide"), P("wide", None), P())
    fits = mesh.shape["wide"] == 16 and mesh.shape["narrow"] == 2
    return jax.shard_map(
        fused_body if fits else body,
        mesh=mesh,
        in_specs=placed,
        out_specs=P("narrow", "wide", None),
        check_vma=False,
    )
```
